32 devices in a mesh: dp: 16 (over z, y, x), mp: 2 (over core).
Axes of the slice: x: 2, y: 2, z: 4, core: 2. Of those that a mesh axis runs over, the one named last changes fastest.
Arguments:
- inputs_blk: bfloat16 [4096, 4, 512], P('dp', 'mp'), may hold values from -6 to 6
- grads_out: bfloat16 [4096, 4, 512], P('dp', 'mp'), may hold values from -0.09375 to 0.09375
- assign: int32 [4], replicated, may hold values from 0 to 1, as said below
- param_owner: int32 [4], replicated, may hold values from 0 to 1, as said below
- left_root: bfloat16 [6, 512, 512], P('mp', 'dp'), as said below
- right_root: bfloat16 [6, 512, 512], P('mp'), as said below
- momentum: float32 [6, 512, 512], P('mp', 'dp'), may hold values from -6 to 6
Outputs:
- new_momentum: float32 [6, 512, 512], P('mp', 'dp')
- update: bfloat16 [6, 512, 512], P('mp', 'dp')
The draws below stay inside these ranges and needn't reach their ends.
Inputs may be any that keep to these rules, and one draw needn't show every extreme that they name: `assign`: no index owns more than 3 blocks, and one owns exactly 3. `param_owner`: no index owns more than 3 blocks, and one owns exactly 3. `left_root`: each matrix is symmetric positive definite. `right_root`: each matrix is symmetric positive definite.
All inputs are finite; a program needn't handle non-finite values.
Results may differ from the reference program's by a relative error of at most 0.0013.
The reference program's roundings to bfloat16 on the way (of `rounded` and `half`) count: a program that leaves them out, or rounds other values in their place, can miss the bound.
Values may be sent and summed in bfloat16 or wider, within the bound.
A program may use at most 64 MiB of HBM per device.

```python
import math
import jax
import jax.numpy as jnp
from jax import lax

B = 512
TOKENS = 4096
NBLK = 4
CAP = 3
SLOTS = 6
N_MP = 2


def hottest_owner(key, owners):
    return jax.random.randint(jax.random.fold_in(key, 77), (), 0, owners).astype(jnp.int32)


def spread_owners(key, blocks, owners, most, hottest):
    order = jax.random.permutation(jax.random.fold_in(key, 1), blocks)
    ranking = jnp.zeros((blocks,), jnp.int32).at[order].set(jnp.arange(blocks, dtype=jnp.int32))
    free_slots = jax.random.permutation(jax.random.fold_in(key, 3), (owners - 1) * most).astype(jnp.int32)
    picked = free_slots[jnp.clip(ranking - most, 0, (owners - 1) * most - 1)]
    others = (hottest + 1 + picked // most) % owners
    return jnp.where(ranking < most, hottest, others).astype(jnp.int32)


def symmetric_root(key, noise):
    level = jax.random.uniform(jax.random.fold_in(key, 5), (N_MP * CAP, 1, 1), jnp.float32, 0.5, 2.0)
    diagonal = jax.random.uniform(jax.random.fold_in(key, 6), (N_MP * CAP, B, 1), jnp.float32, 1.5, 2.5)
    row_ids = lax.broadcasted_iota(jnp.int32, (B, B), 0)
    col_ids = lax.broadcasted_iota(jnp.int32, (B, B), 1)
    mirrored = (noise + jnp.swapaxes(noise, 1, 2)) * (0.35 / math.sqrt(B))
    return (level * jnp.where(row_ids == col_ids, diagonal, mirrored)).astype(jnp.bfloat16)


def draw_assign(key, part):
    hottest = hottest_owner(key, N_MP)
    key = jax.random.fold_in(key, 21)
    return spread_owners(key, NBLK, N_MP, CAP, hottest)


def draw_param_owner(key, part):
    hottest = (hottest_owner(key, N_MP) + 1) % N_MP
    key = jax.random.fold_in(key, 22)
    return spread_owners(key, NBLK, N_MP, CAP, hottest)


def draw_left_root(key, part):
    key = jax.random.fold_in(key, 11)
    shape = (N_MP * CAP, B, B)
    noise = jax.random.normal(jax.random.fold_in(key, 1), shape, jnp.float32)
    return symmetric_root(key, noise)


def draw_right_root(key, part):
    key = jax.random.fold_in(key, 12)
    shape = (N_MP * CAP, B, B)
    noise = jax.random.normal(jax.random.fold_in(key, 1), shape, jnp.float32)
    return symmetric_root(key, noise)


def raised(array, rng, source, target, parts, factor):
    def block_of(axis_at):
        return (jnp.arange(array.shape[axis_at]) // (array.shape[axis_at] // parts)).reshape((-1,) + (1,) * (array.ndim - 1 - axis_at))

    one_side = jax.random.permutation(rng, parts)[block_of(target)]
    far = (block_of(target) + parts // 2) % parts
    return jnp.where((block_of(source) == one_side) | (block_of(source) == far), factor * array, array)


def steps_of(stream_key, shape, cuts, low, top_value):
    level, own = 1.0, jax.random.fold_in(stream_key, 6)
    for axis_at, shards_of in cuts:
        heights = jnp.exp(jax.random.uniform(jax.random.fold_in(own, axis_at), (shards_of,), jnp.float32, low / len(cuts), top_value / len(cuts)))
        level = level * jnp.repeat(heights, shape[axis_at] // shards_of).reshape([-1 if axis == axis_at else 1 for axis in range(len(shape))])
    return level


def normal_values(rng, extent, scale, most, split=(), kind=jnp.bfloat16):
    drawn = jax.random.normal(rng, extent, jnp.float32) * scale
    if len(split) > 0:
        drawn = steps_of(rng, extent, split, -0.22, 0.18) * drawn
    return jnp.clip(drawn, min=-most, max=most).astype(kind)


def bell_draw_with(key, shape, spread, limit, pieces, heavy, kind=jnp.bfloat16):
    entries = spread * jax.random.normal(key, shape, jnp.float32)
    if pieces:
        entries = entries * steps_of(key, shape, pieces, -0.22, 0.18)
    return jnp.clip(raised(entries, jax.random.fold_in(key, 3), *heavy), -limit, limit).astype(kind)


def setup_inputs(seed: int = 0) -> dict:
    keys = jax.random.split(jax.random.key(seed), 8)
    return {
        "inputs_blk": bell_draw_with(keys[0], (TOKENS, NBLK, B), 1.0, 6.0, ((0, 16), (1, 2)), (0, 2, 16, 2.0)),
        "grads_out": normal_values(keys[1], (TOKENS, NBLK, B), TOKENS ** -0.5, 0.09375, ((0, 16), (1, 2))),
        "assign": draw_assign(jax.random.fold_in(keys[7], 71), 0),
        "param_owner": draw_param_owner(jax.random.fold_in(keys[7], 71), 0),
        "left_root": draw_left_root(jax.random.fold_in(keys[7], 71), 0),
        "right_root": draw_right_root(jax.random.fold_in(keys[7], 71), 0),
        "momentum": normal_values(keys[6], (SLOTS, B, B), 1.0, 6.0, ((0, 2), (1, 16)), jnp.float32),
    }


BETA = 0.9
EPS = 1e-06

def slots_of(owners):
    block_ids = jnp.arange(owners.shape[0], dtype=jnp.int32)
    same = (owners[None, :] == owners[:, None]) & (block_ids[None, :] < block_ids[:, None])
    return lax.optimization_barrier(jnp.sum(same.astype(jnp.int32), axis=1)).astype(jnp.int32)

def reference(inputs_blk, grads_out, assign, param_owner, left_root, right_root, momentum):
    slot = slots_of(assign)
    place = slots_of(param_owner)
    new_momentum = BETA * momentum
    update = jnp.zeros((N_MP * CAP, B, B), jnp.bfloat16)
    for block in range(NBLK):
        grad = jnp.dot(inputs_blk[:, block, :].T, grads_out[:, block, :], preferred_element_type=jnp.float32)
        rounded = grad.astype(jnp.bfloat16)
        index = (assign[block] * CAP + slot[block]).astype(jnp.int32)
        half = jnp.dot(rounded, right_root[index], preferred_element_type=jnp.float32).astype(jnp.bfloat16)
        both = jnp.dot(left_root[index], half, preferred_element_type=jnp.float32)
        grad_square = jnp.sum(jnp.square(rounded.astype(jnp.float32)))
        prec_square = jnp.sum(both * both)
        grafted = both * jnp.sqrt(grad_square / (prec_square + EPS))
        moved = BETA * momentum[index] + grafted
        new_momentum = new_momentum.at[index].set(moved)
        target = (param_owner[block] * CAP + place[block]).astype(jnp.int32)
        update = update.at[target].set(moved.astype(jnp.bfloat16))
    return (new_momentum, update)
```

```python
import functools

import jax
import jax.numpy as jnp
from jax import lax
from jax.experimental import pallas as pl
from jax.experimental.pallas import tpu as pltpu
from jax.sharding import PartitionSpec as P

BETA = 0.9
EPS = 1e-06
QUAD = 4
PARTS = 2
MESH = pl.DeviceIdType.MESH
F32 = jnp.float32
BF16 = jnp.bfloat16


def slots_of(owners):
    block_ids = jnp.arange(owners.shape[0], dtype=jnp.int32)
    same = (owners[None, :] == owners[:, None]) & (block_ids[None, :] < block_ids[:, None])
    return jnp.sum(same.astype(jnp.int32), axis=1)


def scalar_places(ref, blocks, capacity):
    owners = [ref[k] for k in range(blocks)]
    places = []
    for k in range(blocks):
        count = owners[k] * capacity
        for j in range(k):
            count = count + jnp.where(owners[j] == owners[k], 1, 0)
        places.append(count)
    return places


def hot(a, b):
    return jnp.where(a == b, 1.0, 0.0).astype(F32)


def kernel(
    dims,
    x_ref, y_ref, assign_ref, owner_ref, left_hbm, right_hbm, mom_hbm,
    mom_out, upd_out,
    g_ref, r1_ref, t_ref, r2_ref, full_ref, right_ref, left_ref, mom_ref,
    rsel_ref, lsel_ref, msel_ref, both_ref, p_ref, pr_ref,
    local_sem, pre_send, pre_recv, s1_send, s1_recv, s2_send, s2_recv, s3_send, s3_recv,
    s4_send, s4_recv, fw_send, fw_recv, p_send, p_recv,
):
    n_dp, mine, blocks, capacity, size = dims
    lines = n_dp // QUAD
    rows = size // n_dp
    band = size // QUAD
    width = size // PARTS
    chunks = mine * PARTS
    me = lax.axis_index("dp")
    core = lax.axis_index("mp")
    q = lax.rem(me, QUAD)
    z = me // QUAD
    other = 1 - core

    def at_quad(j):
        return (z * QUAD + lax.rem(q + j, QUAD), core)

    def at_line(j):
        return (lax.rem(z + j, lines) * QUAD + q, core)

    barrier = pltpu.get_barrier_semaphore()
    for j in range(1, n_dp):
        pl.semaphore_signal(barrier, inc=1, device_id=(lax.rem(me + j, n_dp), core), device_id_type=MESH)
    pl.semaphore_signal(barrier, inc=1, device_id=(me, other), device_id_type=MESH)

    own = pl.ds(core * capacity, capacity)
    theirs = pl.ds(other * capacity, capacity)
    stored = ((right_hbm, right_ref), (left_hbm, left_ref), (mom_hbm, mom_ref))
    local = [
        pltpu.make_async_copy(src, dst.at[own], local_sem.at[i]) for i, (src, dst) in enumerate(stored)
    ]
    for copy in local:
        copy.start()

    def multiply(c):
        k, h = divmod(c, PARTS)
        x = x_ref[:, k * size:(k + 1) * size]
        y = y_ref[:, k * size + h * width:k * size + (h + 1) * width]
        g_ref[c] = lax.dot_general(x, y, (((0,), (0,)), ((), ())), preferred_element_type=F32)

    sends = []

    def remote(src, dst, send, recv, device):
        return pltpu.make_async_remote_copy(
            src_ref=src, dst_ref=dst, send_sem=send, recv_sem=recv, device_id=device, device_id_type=MESH
        )

    def start(copy):
        copy.start()
        sends.append(copy)

    def s1(c):
        for j in range(1, QUAD):
            band_at = pl.ds(lax.rem(q + j, QUAD) * band, band)
            start(remote(g_ref.at[c, band_at], r1_ref.at[c, j - 1], s1_send.at[c, j - 1], s1_recv.at[c, j - 1], at_quad(j)))

    def s2(c):
        for j in range(1, QUAD):
            remote(r1_ref.at[c, j - 1], r1_ref.at[c, j - 1], s1_send.at[c, j - 1], s1_recv.at[c, j - 1], at_quad(j)).wait_recv()
        total = g_ref[c, pl.ds(q * band, band), :]
        for j in range(1, QUAD):
            total = total + r1_ref[c, j - 1]
        t_ref[c] = total
        for j in range(1, lines):
            rows_at = pl.ds(lax.rem(z + j, lines) * rows, rows)
            start(remote(t_ref.at[c, rows_at], r2_ref.at[c, j - 1], s2_send.at[c, j - 1], s2_recv.at[c, j - 1], at_line(j)))

    def s3(c):
        for j in range(1, lines):
            remote(r2_ref.at[c, j - 1], r2_ref.at[c, j - 1], s2_send.at[c, j - 1], s2_recv.at[c, j - 1], at_line(j)).wait_recv()
        total = t_ref[c, pl.ds(z * rows, rows), :]
        for j in range(1, lines):
            total = total + r2_ref[c, j - 1]
        g = core * chunks + c
        mine_at = pl.ds(q * band + z * rows, rows)
        full_ref[g, mine_at, :] = total.astype(BF16)
        piece = full_ref.at[g, mine_at]
        for j in range(1, lines):
            start(remote(piece, piece, s3_send.at[c, j - 1], s3_recv.at[c, j - 1], at_line(j)))

    def s4(c):
        g = core * chunks + c
        for j in range(1, lines):
            source = lax.rem(z + lines - j, lines)
            piece = full_ref.at[g, pl.ds(q * band + source * rows, rows)]
            remote(piece, piece, s3_send.at[c, j - 1], s3_recv.at[c, j - 1], at_line(j)).wait_recv()
        piece = full_ref.at[g, pl.ds(q * band, band)]
        for j in range(1, QUAD):
            start(remote(piece, piece, s4_send.at[c, j - 1], s4_recv.at[c, j - 1], at_quad(j)))
        start(remote(piece, piece, fw_send.at[c, 0], fw_recv.at[c, 0], (me, other)))

    def s5(c):
        g = core * chunks + c
        for j in range(1, QUAD):
            source = lax.rem(q + QUAD - j, QUAD)
            piece = full_ref.at[g, pl.ds(source * band, band)]
            remote(piece, piece, s4_send.at[c, j - 1], s4_recv.at[c, j - 1], at_quad(j)).wait_recv()
            start(remote(piece, piece, fw_send.at[c, j], fw_recv.at[c, j], (me, other)))

    def s6(c):
        g = other * chunks + c
        for j in range(QUAD):
            source = lax.rem(q + QUAD - j, QUAD)
            piece = full_ref.at[g, pl.ds(source * band, band)]
            remote(piece, piece, fw_send.at[c, j], fw_recv.at[c, j], (me, other)).wait_recv()

    multiply(0)
    pl.semaphore_wait(barrier, n_dp)
    s1(0)
    for c in range(1, chunks):
        multiply(c)
        s1(c)
    for i, (src, dst) in enumerate(stored):
        start(remote(src, dst.at[own], pre_send.at[i], pre_recv.at[i], (me, other)))

    index = scalar_places(assign_ref, blocks, capacity)
    target = scalar_places(owner_ref, blocks, capacity)
    for copy in local:
        copy.wait()
    for i, (src, dst) in enumerate(stored):
        remote(src, dst.at[theirs], pre_send.at[i], pre_recv.at[i], (me, other)).wait_recv()

    slots = 2 * capacity
    for k in range(blocks):
        picks = [hot(index[k], s) for s in range(slots)]

        def pick(at, _, k=k, picks=picks):
            part = pl.ds(pl.multiple_of(at * 64, 64), 64)
            chosen = right_ref[0, part, :].astype(F32) * picks[0]
            for s in range(1, slots):
                chosen = chosen + right_ref[s, part, :].astype(F32) * picks[s]
            rsel_ref[k, part, :] = chosen.astype(BF16)
            return 0

        lax.fori_loop(0, size // 64, pick, 0)
        chosen = left_ref[0].astype(F32) * picks[0]
        moment = mom_ref[0] * picks[0]
        for s in range(1, slots):
            chosen = chosen + left_ref[s].astype(F32) * picks[s]
            moment = moment + mom_ref[s] * picks[s]
        lsel_ref[k] = chosen.astype(BF16)
        msel_ref[k] = moment

    stages = (s2, s3, s4, s5)
    for step in range(chunks + len(stages) - 1):
        for late in reversed(range(len(stages))):
            c = step - late
            if 0 <= c < chunks:
                stages[late](c)
    for c in range(chunks):
        s6(c)

    def precondition(k, _):
        half = jnp.zeros((size, size), F32)
        for h in range(PARTS):
            half = half + jnp.dot(
                full_ref[k * PARTS + h], rsel_ref[k, h * width:(h + 1) * width, :], preferred_element_type=F32
            )
        both_ref[k] = jnp.dot(lsel_ref[k], half.astype(BF16), preferred_element_type=F32)
        return 0

    lax.fori_loop(0, blocks, precondition, 0)

    def lanes(value):
        partial = value[:, 0:128]
        for at in range(128, value.shape[1], 128):
            partial = partial + value[:, at:at + 128]
        return jnp.sum(partial, axis=0, keepdims=True)

    p_ref[...] = jnp.zeros_like(p_ref)
    for k in range(blocks):
        both = both_ref[k]
        p_ref[k:k + 1, :] = lanes(both * both)
    for j in range(1, n_dp):
        start(remote(p_ref, pr_ref.at[j - 1], p_send.at[j - 1], p_recv.at[j - 1], (lax.rem(me + j, n_dp), core)))

    grad_square = []
    for k in range(blocks):
        def add(at, total, k=k):
            part = pl.ds(pl.multiple_of(at * 64, 64), 64)
            for h in range(PARTS):
                value = full_ref[k * PARTS + h, part, :].astype(F32)
                total = total + lanes(value * value)
            return total

        lane_sum = lax.fori_loop(0, size // 64, add, jnp.zeros((1, 128), F32))
        grad_square.append(jnp.sum(lane_sum, axis=1, keepdims=True))

    for j in range(1, n_dp):
        remote(p_ref, pr_ref.at[j - 1], p_send.at[j - 1], p_recv.at[j - 1], (lax.rem(me + j, n_dp), core)).wait_recv()
    total = p_ref[...]
    for j in range(1, n_dp):
        total = total + pr_ref[j - 1]
    prec_square = jnp.sum(total, axis=1, keepdims=True)
    grafted = [
        both_ref[k] * jnp.sqrt(grad_square[k] / (prec_square[k:k + 1, :] + EPS)) for k in range(blocks)
    ]
    moved = [(BETA * msel_ref[k] + grafted[k]).astype(BF16).astype(F32) for k in range(blocks)]
    for s in range(capacity):
        here = core * capacity + s
        value = BETA * mom_ref[here]
        update = jnp.zeros((rows, size), F32)
        for k in range(blocks):
            value = value + grafted[k] * hot(index[k], here)
            update = update + moved[k] * hot(target[k], here)
        mom_out[s] = value
        upd_out[s] = update.astype(BF16)
    for copy in sends:
        copy.wait_send()


def fused(n_dp, inputs_blk, grads_out, assign, param_owner, left_root, right_root, momentum):
    tokens, mine, size = inputs_blk.shape
    capacity = right_root.shape[0]
    blocks = assign.shape[0]
    rows = size // n_dp
    band, width, lines = size // QUAD, size // PARTS, n_dp // QUAD
    chunks = mine * PARTS
    slots = 2 * capacity
    vmem = pl.BlockSpec(memory_space=pltpu.VMEM)
    smem = pl.BlockSpec(memory_space=pltpu.SMEM)
    anyw = pl.BlockSpec(memory_space=pl.ANY)
    dma = pltpu.SemaphoreType.DMA
    flops = 2 * mine * tokens * size * size + 2 * blocks * size**3
    return pl.pallas_call(
        functools.partial(kernel, (n_dp, mine, blocks, capacity, size)),
        out_shape=(
            jax.ShapeDtypeStruct((capacity, rows, size), F32),
            jax.ShapeDtypeStruct((capacity, rows, size), BF16),
        ),
        in_specs=[vmem, vmem, smem, smem, anyw, anyw, anyw],
        out_specs=(vmem, vmem),
        scratch_shapes=[
            pltpu.VMEM((chunks, size, width), F32),
            pltpu.VMEM((chunks, QUAD - 1, band, width), F32),
            pltpu.VMEM((chunks, band, width), F32),
            pltpu.VMEM((chunks, lines - 1, rows, width), F32),
            pltpu.VMEM((2 * chunks, size, width), BF16),
            pltpu.VMEM((slots, size, size), BF16),
            pltpu.VMEM((slots, rows, size), BF16),
            pltpu.VMEM((slots, rows, size), F32),
            pltpu.VMEM((blocks, size, size), BF16),
            pltpu.VMEM((blocks, rows, size), BF16),
            pltpu.VMEM((blocks, rows, size), F32),
            pltpu.VMEM((blocks, rows, size), F32),
            pltpu.VMEM((8, 128), F32),
            pltpu.VMEM((n_dp - 1, 8, 128), F32),
            dma((3,)), dma((3,)), dma((3,)),
            dma((chunks, QUAD - 1)), dma((chunks, QUAD - 1)),
            dma((chunks, lines - 1)), dma((chunks, lines - 1)),
            dma((chunks, lines - 1)), dma((chunks, lines - 1)),
            dma((chunks, QUAD - 1)), dma((chunks, QUAD - 1)),
            dma((chunks, QUAD)), dma((chunks, QUAD)),
            dma((n_dp - 1,)), dma((n_dp - 1,)),
        ],
        compiler_params=pltpu.CompilerParams(
            collective_id=0, has_side_effects=True, vmem_limit_bytes=40 * 1024 * 1024
        ),
        cost_estimate=pl.CostEstimate(flops=flops, bytes_accessed=4 * 1024 * 1024, transcendentals=0),
    )(
        inputs_blk.reshape(tokens, mine * size),
        grads_out.reshape(tokens, mine * size),
        assign, param_owner, left_root, right_root, momentum,
    )


def general(inputs_blk, grads_out, assign, param_owner, left_root, right_root, momentum):
    capacity = right_root.shape[0]
    blocks = assign.shape[0]
    my_index = lax.axis_index("mp")
    reduced = lax.psum_scatter(
        jnp.einsum("tkr,tkc->rkc", inputs_blk, grads_out, preferred_element_type=F32),
        "dp",
        scatter_dimension=0,
        tiled=True,
    )
    rounded = reduced.astype(BF16)
    gathered = lax.all_gather(rounded, "mp", axis=1, tiled=True)
    slot = slots_of(assign)
    slot_ids = lax.broadcasted_iota(jnp.int32, (capacity, blocks), 0)
    chooser = ((assign[None, :] == my_index) & (slot[None, :] == slot_ids)).astype(BF16)
    owned = jnp.einsum("ck,rkb->crb", chooser, gathered, preferred_element_type=F32).astype(BF16)
    half = jnp.einsum("crb,cbe->cre", owned, right_root, preferred_element_type=F32).astype(BF16)
    both = jnp.einsum(
        "cri,cie->cre",
        left_root,
        lax.all_gather(half, "dp", axis=1, tiled=True),
        preferred_element_type=F32,
    )
    grad_square = jnp.sum(jnp.square(owned.astype(F32)), axis=(1, 2))
    prec_square = jnp.sum(both * both, axis=(1, 2))
    grad_square, prec_square = lax.psum((grad_square, prec_square), "dp")
    factor = jnp.sqrt(grad_square / (prec_square + EPS))
    moved = BETA * momentum + both * factor[:, None, None]
    sending = moved.astype(BF16)
    pooled = lax.all_gather(sending, "mp", axis=0, tiled=True)
    place = slots_of(param_owner)
    source = assign * capacity + slot
    target_hot = ((param_owner[None, :] == my_index) & (place[None, :] == slot_ids)).astype(F32)
    pool_ids = lax.broadcasted_iota(jnp.int32, (blocks, pooled.shape[0]), 1)
    source_hot = (source[:, None] == pool_ids).astype(F32)
    mover = jnp.dot(target_hot, source_hot, preferred_element_type=F32).astype(BF16)
    update = jnp.einsum("qs,srb->qrb", mover, pooled, preferred_element_type=F32).astype(BF16)
    return (moved, update)


def solution(mesh):
    n_dp, n_mp = mesh.shape["dp"], mesh.shape["mp"]

    def on_device(inputs_blk, *rest):
        rows = inputs_blk.shape[2] // n_dp
        if n_mp == 2 and n_dp % QUAD == 0 and rows % 16 == 0:
            return fused(n_dp, inputs_blk, *rest)
        return general(inputs_blk, *rest)

    placed = (
        P("dp", "mp", None),
        P("dp", "mp", None),
        P(),
        P(),
        P("mp", "dp", None),
        P("mp", None, None),
        P("mp", "dp", None),
    )
    return jax.shard_map(
        on_device,
        mesh=mesh,
        in_specs=placed,
        out_specs=(P("mp", "dp", None), P("mp", "dp", None)),
        check_vma=False,
    )
```

```python
import functools

import jax
import jax.numpy as jnp
from jax import lax
from jax.experimental import pallas as pl
from jax.experimental.pallas import tpu as pltpu
from jax.sharding import PartitionSpec as P

BETA = 0.9
EPS = 1e-06
PLANE = 4
PARTS = 2
MESH = pl.DeviceIdType.MESH
F32 = jnp.float32
BF16 = jnp.bfloat16


def slots_of(owners):
    block_ids = jnp.arange(owners.shape[0], dtype=jnp.int32)
    same = (owners[None, :] == owners[:, None]) & (block_ids[None, :] < block_ids[:, None])
    return jnp.sum(same.astype(jnp.int32), axis=1)


def scalar_places(ref, blocks, capacity):
    owners = [ref[k] for k in range(blocks)]
    places = []
    for k in range(blocks):
        count = owners[k] * capacity
        for j in range(k):
            count = count + jnp.where(owners[j] == owners[k], 1, 0)
        places.append(count)
    return places


def hot(a, b):
    return jnp.where(a == b, 1.0, 0.0).astype(F32)


def kernel(
    dims,
    x_ref, y_ref, assign_ref, owner_ref, left_hbm, right_hbm, mom_hbm,
    mom_out, upd_out,
    xr_ref, yr_ref, g_ref, r1_ref, t_ref, r2_ref, own_ref, right_ref, left_ref, mom_ref,
    rsel_ref, lband_ref, msel_ref, hb_ref, hall_ref, hfull_ref, bo_ref, both_ref, p_ref, pr_ref, sum_ref,
    local_sem, pre_send, pre_recv, x_send, x_recv, y_send, y_recv, s1_send, s1_recv, s2_send, s2_recv,
    left_send, left_recv, half_send, half_recv, both_send, both_recv, fw_send, fw_recv,
    p_send, p_recv, sum_send, sum_recv,
):
    n_dp, mine, blocks, capacity, size = dims
    lines = n_dp // PLANE
    rows = size // n_dp
    band = size // PLANE
    wing = size // 2
    width = size // PARTS
    me = lax.axis_index("dp")
    core = lax.axis_index("mp")
    q = lax.rem(me, PLANE)
    z = me // PLANE
    x_at, y_at = lax.rem(q, 2), q // 2
    other = 1 - core
    x_mate = (z * PLANE + y_at * 2 + (1 - x_at), core)
    y_mate = (z * PLANE + (1 - y_at) * 2 + x_at, core)
    core_mate = (me, other)

    def plane_mate(j):
        return (z * PLANE + lax.rem(q + j, PLANE), core)

    routes = [
        (x_at, y_at, x_mate, y_mate) if k % 2 == 0 else (y_at, x_at, y_mate, x_mate) for k in range(mine)
    ]

    def at_line(j):
        return (lax.rem(z + j, lines) * PLANE + q, core)

    barrier = pltpu.get_barrier_semaphore()
    partners = [x_mate, y_mate, core_mate] + [at_line(j) for j in range(1, lines)]
    for device in partners:
        pl.semaphore_signal(barrier, inc=1, device_id=device, device_id_type=MESH)

    own = pl.ds(core * capacity, capacity)
    theirs = pl.ds(other * capacity, capacity)
    stored = ((right_hbm, right_ref), (left_hbm, left_ref), (mom_hbm, mom_ref))
    local = [
        pltpu.make_async_copy(src, dst.at[own], local_sem.at[i]) for i, (src, dst) in enumerate(stored)
    ]
    for copy in local:
        copy.start()

    sends = []

    def remote(src, dst, send, recv, device):
        return pltpu.make_async_remote_copy(
            src_ref=src, dst_ref=dst, send_sem=send, recv_sem=recv, device_id=device, device_id_type=MESH
        )

    def start(copy):
        copy.start()
        sends.append(copy)

    def outer(x, y):
        return lax.dot_general(x, y, (((0,), (0,)), ((), ())), preferred_element_type=F32)

    def cols(h):
        return slice(h * width, (h + 1) * width)

    def wing_of(k, a):
        return pl.ds(pl.multiple_of(k * size + a * wing, wing), wing)

    def x_copy(k):
        a, _, mate, _ = routes[k]
        return remote(x_ref.at[:, wing_of(k, 1 - a)], xr_ref.at[k], x_send.at[k], x_recv.at[k], mate)

    def y_copy(k, h):
        src = y_ref.at[:, pl.ds(k * size + h * width, width)]
        return remote(src, yr_ref.at[k, :, pl.ds(h * width, width)], y_send.at[k, h], y_recv.at[k, h], routes[k][2])

    def wing_copy(k, h):
        _, b, _, mate = routes[k]
        src = g_ref.at[k, pl.ds((1 - b) * band, band), pl.ds(h * width, width)]
        return remote(src, r1_ref.at[k, :, pl.ds(h * width, width)], s1_send.at[k, h], s1_recv.at[k, h], mate)

    def line_copy(k, h, j):
        src = t_ref.at[k, pl.ds(lax.rem(z + j, lines) * rows, rows), pl.ds(h * width, width)]
        dst = r2_ref.at[k, j - 1, :, pl.ds(h * width, width)]
        return remote(src, dst, s2_send.at[k, h, j - 1], s2_recv.at[k, h, j - 1], at_line(j))

    def s1(k, h):
        if h == 0:
            x_copy(k).wait_recv()
        y_copy(k, h).wait_recv()
        g_ref[k, :, cols(h)] = g_ref[k, :, cols(h)] + outer(xr_ref[k], yr_ref[k, :, cols(h)])
        start(wing_copy(k, h))

    def s2(k, h):
        b = routes[k][1]
        wing_copy(k, h).wait_recv()
        t_ref[k, :, cols(h)] = g_ref[k, pl.ds(b * band, band), cols(h)] + r1_ref[k, :, cols(h)]
        for j in range(1, lines):
            start(line_copy(k, h, j))

    def s3(k, h):
        total = t_ref[k, pl.ds(z * rows, rows), cols(h)]
        for j in range(1, lines):
            line_copy(k, h, j).wait_recv()
            total = total + r2_ref[k, j - 1, :, cols(h)]
        own_ref[k, :, cols(h)] = total.astype(BF16)

    pl.semaphore_wait(barrier, len(partners))
    for k in range(mine):
        start(x_copy(k))
    for h in range(PARTS):
        for k in range(mine):
            start(y_copy(k, h))
    for i, (src, dst) in enumerate(stored):
        start(remote(src, dst.at[own], pre_send.at[i], pre_recv.at[i], core_mate))
    for k in range(mine):
        g_ref[k] = outer(x_ref[:, wing_of(k, routes[k][0])], y_ref[:, k * size:(k + 1) * size])

    index = scalar_places(assign_ref, blocks, capacity)
    target = scalar_places(owner_ref, blocks, capacity)
    slots = 2 * capacity

    local_index = [jnp.where(core == 0, index[k], index[mine + k]) for k in range(mine)]

    def select():
        for copy in local:
            copy.wait()
        for i, (src, dst) in enumerate(stored):
            remote(src, dst.at[theirs], pre_send.at[i], pre_recv.at[i], core_mate).wait_recv()
        for k in range(mine):
            picks = [hot(local_index[k], s) for s in range(slots)]

            def pick(at, _, k=k, picks=picks):
                part = pl.ds(pl.multiple_of(at * 64, 64), 64)
                chosen = right_ref[0, part, :].astype(F32) * picks[0]
                for s in range(1, slots):
                    chosen = chosen + right_ref[s, part, :].astype(F32) * picks[s]
                rsel_ref[k, part, :] = chosen.astype(BF16)
                return 0

            lax.fori_loop(0, size // 64, pick, 0)
            chosen = left_ref[0].astype(F32) * picks[0]
            for s in range(1, slots):
                chosen = chosen + left_ref[s].astype(F32) * picks[s]
            lband_ref[q, k] = chosen.astype(BF16)
        for k in range(blocks):
            moment = mom_ref[0] * hot(index[k], 0)
            for s in range(1, slots):
                moment = moment + mom_ref[s] * hot(index[k], s)
            msel_ref[k] = moment

    def left_copy(j, place):
        part = lband_ref.at[place]
        return remote(part, part, left_send.at[j - 1], left_recv.at[j - 1], plane_mate(j))

    def half_copy(j, place):
        device = lax.rem(me + j, n_dp)
        src = hb_ref.at[lax.rem(device, PLANE)]
        return remote(src, hall_ref.at[place], half_send.at[j - 1], half_recv.at[j - 1], (device, core))

    def both_copy(j, place):
        src = bo_ref.at[lax.rem(q + j, PLANE)]
        return remote(src, both_ref.at[core, place], both_send.at[j - 1], both_recv.at[j - 1], plane_mate(j))

    def core_copy(j, at):
        part = both_ref.at[at, lax.rem(q + PLANE - j, PLANE)]
        return remote(part, part, fw_send.at[j], fw_recv.at[j], core_mate)

    def p_copy(j):
        device = (lax.rem(me + j, n_dp), core)
        return remote(p_ref, pr_ref.at[j - 1], p_send.at[j - 1], p_recv.at[j - 1], device)

    def lanes(value):
        partial = value[:, 0:128]
        for at in range(128, value.shape[1], 128):
            partial = partial + value[:, at:at + 128]
        return jnp.sum(partial, axis=0, keepdims=True)

    order = [(k, h) for h in range(PARTS) for k in range(mine)]
    stages = (s1, s2, s3)
    for step in range(len(order) + len(stages) - 1):
        for late in range(len(stages)):
            if 0 <= step - late < len(order):
                stages[late](*order[step - late])
        if step == 1:
            select()
        if step == len(order):
            for j in range(1, PLANE):
                left_copy(j, q).start()

    p_ref[...] = jnp.zeros_like(p_ref)
    for k in range(mine):
        half = jnp.dot(own_ref[k], rsel_ref[k], preferred_element_type=F32).astype(BF16)
        for j in range(PLANE):
            hb_ref[j, k] = half[:, j * band:(j + 1) * band]
    for j in range(1, n_dp):
        half_copy(j, me).start()
    hall_ref[me] = hb_ref[q]
    for k in range(mine):
        value = own_ref[k].astype(F32)
        p_ref[mine + k:mine + k + 1, :] = lanes(value * value)
    for j in range(1, PLANE):
        left_copy(j, lax.rem(q + PLANE - j, PLANE)).wait_recv()
    for j in range(1, n_dp):
        half_copy(j, lax.rem(me + n_dp - j, n_dp)).wait_recv()
    for device in range(n_dp):
        line, corner = divmod(device, PLANE)
        for k in range(mine):
            a, b = (corner % 2, corner // 2) if k % 2 == 0 else (corner // 2, corner % 2)
            first = (a * 2 + b) * band + line * rows
            hfull_ref[k, first:first + rows, :] = hall_ref[device, k]
    for k in range(mine):
        square = jnp.zeros((1, 128), F32)
        for j in range(PLANE):
            value = jnp.dot(lband_ref[j, k], hfull_ref[k], preferred_element_type=F32)
            bo_ref[j, k] = value
            square = square + lanes(value * value)
        p_ref[k:k + 1, :] = square
    for j in range(1, n_dp):
        p_copy(j).start()
    for j in range(1, PLANE):
        both_copy(j, q).start()
    both_ref[core, q] = bo_ref[q]
    core_copy(0, core).start()
    for j in range(1, PLANE):
        both_copy(j, lax.rem(q + PLANE - j, PLANE)).wait_recv()
        core_copy(j, core).start()
    total = p_ref[...]
    for j in range(1, n_dp):
        p_copy(j).wait_recv()
        total = total + pr_ref[j - 1]
    sum_ref[core] = total
    sum_mine, sum_theirs = sum_ref.at[core], sum_ref.at[other]
    remote(sum_mine, sum_mine, sum_send.at[0], sum_recv.at[0], core_mate).start()
    for j in range(PLANE):
        core_copy(j, other).wait_recv()
    remote(sum_theirs, sum_theirs, sum_send.at[0], sum_recv.at[0], core_mate).wait_recv()

    factors = []
    for k in range(blocks):
        sums = jnp.sum(sum_ref[k // mine], axis=1, keepdims=True)
        at = k % mine
        factors.append(jnp.sqrt(sums[mine + at:mine + at + 1] / (sums[at:at + 1] + EPS)))
    for j in range(PLANE):
        part = slice(j * band, (j + 1) * band)
        grafted = [both_ref[k // mine, j, k % mine] * factors[k] for k in range(blocks)]
        moved = [(BETA * msel_ref[k, :, part] + grafted[k]).astype(BF16).astype(F32) for k in range(blocks)]
        for s in range(capacity):
            here = core * capacity + s
            value = BETA * mom_ref[here, :, part]
            update = jnp.zeros((rows, band), F32)
            for k in range(blocks):
                value = value + grafted[k] * hot(index[k], here)
                update = update + moved[k] * hot(target[k], here)
            mom_out[s, :, part] = value
            upd_out[s, :, part] = update.astype(BF16)
    for j in range(1, PLANE):
        left_copy(j, q).wait_send()
        both_copy(j, q).wait_send()
    for j in range(1, n_dp):
        half_copy(j, me).wait_send()
        p_copy(j).wait_send()
    for j in range(PLANE):
        core_copy(j, core).wait_send()
    remote(sum_mine, sum_mine, sum_send.at[0], sum_recv.at[0], core_mate).wait_send()
    for copy in sends:
        copy.wait_send()


def fused(n_dp, inputs_blk, grads_out, assign, param_owner, left_root, right_root, momentum):
    tokens, mine, size = inputs_blk.shape
    capacity = right_root.shape[0]
    blocks = assign.shape[0]
    rows = size // n_dp
    band, wing, lines = size // PLANE, size // 2, n_dp // PLANE
    slots = 2 * capacity
    vmem = pl.BlockSpec(memory_space=pltpu.VMEM)
    smem = pl.BlockSpec(memory_space=pltpu.SMEM)
    anyw = pl.BlockSpec(memory_space=pl.ANY)
    dma = pltpu.SemaphoreType.DMA
    flops = 2 * mine * tokens * size * size + 2 * blocks * size**3
    return pl.pallas_call(
        functools.partial(kernel, (n_dp, mine, blocks, capacity, size)),
        out_shape=(
            jax.ShapeDtypeStruct((capacity, rows, size), F32),
            jax.ShapeDtypeStruct((capacity, rows, size), BF16),
        ),
        in_specs=[vmem, vmem, smem, smem, anyw, anyw, anyw],
        out_specs=(vmem, vmem),
        scratch_shapes=[
            pltpu.VMEM((mine, tokens, wing), BF16),
            pltpu.VMEM((mine, tokens, size), BF16),
            pltpu.VMEM((mine, wing, size), F32),
            pltpu.VMEM((mine, band, size), F32),
            pltpu.VMEM((mine, band, size), F32),
            pltpu.VMEM((mine, lines - 1, rows, size), F32),
            pltpu.VMEM((mine, rows, size), BF16),
            pltpu.VMEM((slots, size, size), BF16),
            pltpu.VMEM((slots, rows, size), BF16),
            pltpu.VMEM((slots, rows, size), F32),
            pltpu.VMEM((mine, size, size), BF16),
            pltpu.VMEM((PLANE, mine, rows, size), BF16),
            pltpu.VMEM((blocks, rows, size), F32),
            pltpu.VMEM((PLANE, mine, rows, band), BF16),
            pltpu.VMEM((n_dp, mine, rows, band), BF16),
            pltpu.VMEM((mine, size, band), BF16),
            pltpu.VMEM((PLANE, mine, rows, band), F32),
            pltpu.VMEM((2, PLANE, mine, rows, band), F32),
            pltpu.VMEM((8, 128), F32),
            pltpu.VMEM((n_dp - 1, 8, 128), F32),
            pltpu.VMEM((2, 8, 128), F32),
            dma((3,)), dma((3,)), dma((3,)),
            dma((mine,)), dma((mine,)),
            dma((mine, PARTS)), dma((mine, PARTS)),
            dma((mine, PARTS)), dma((mine, PARTS)),
            dma((mine, PARTS, lines - 1)), dma((mine, PARTS, lines - 1)),
            dma((PLANE - 1,)), dma((PLANE - 1,)),
            dma((n_dp - 1,)), dma((n_dp - 1,)),
            dma((PLANE - 1,)), dma((PLANE - 1,)),
            dma((PLANE,)), dma((PLANE,)),
            dma((n_dp - 1,)), dma((n_dp - 1,)),
            dma((1,)), dma((1,)),
        ],
        compiler_params=pltpu.CompilerParams(
            collective_id=0, has_side_effects=True, vmem_limit_bytes=40 * 1024 * 1024
        ),
        cost_estimate=pl.CostEstimate(flops=flops, bytes_accessed=4 * 1024 * 1024, transcendentals=0),
    )(
        inputs_blk.reshape(tokens, mine * size),
        grads_out.reshape(tokens, mine * size),
        assign, param_owner, left_root, right_root, momentum,
    )


def general(inputs_blk, grads_out, assign, param_owner, left_root, right_root, momentum):
    capacity = right_root.shape[0]
    blocks = assign.shape[0]
    my_index = lax.axis_index("mp")
    reduced = lax.psum_scatter(
        jnp.einsum("tkr,tkc->rkc", inputs_blk, grads_out, preferred_element_type=F32),
        "dp",
        scatter_dimension=0,
        tiled=True,
    )
    rounded = reduced.astype(BF16)
    gathered = lax.all_gather(rounded, "mp", axis=1, tiled=True)
    slot = slots_of(assign)
    slot_ids = lax.broadcasted_iota(jnp.int32, (capacity, blocks), 0)
    chooser = ((assign[None, :] == my_index) & (slot[None, :] == slot_ids)).astype(BF16)
    owned = jnp.einsum("ck,rkb->crb", chooser, gathered, preferred_element_type=F32).astype(BF16)
    half = jnp.einsum("crb,cbe->cre", owned, right_root, preferred_element_type=F32).astype(BF16)
    both = jnp.einsum(
        "cri,cie->cre",
        left_root,
        lax.all_gather(half, "dp", axis=1, tiled=True),
        preferred_element_type=F32,
    )
    grad_square = jnp.sum(jnp.square(owned.astype(F32)), axis=(1, 2))
    prec_square = jnp.sum(both * both, axis=(1, 2))
    grad_square, prec_square = lax.psum((grad_square, prec_square), "dp")
    factor = jnp.sqrt(grad_square / (prec_square + EPS))
    moved = BETA * momentum + both * factor[:, None, None]
    sending = moved.astype(BF16)
    pooled = lax.all_gather(sending, "mp", axis=0, tiled=True)
    place = slots_of(param_owner)
    source = assign * capacity + slot
    target_hot = ((param_owner[None, :] == my_index) & (place[None, :] == slot_ids)).astype(F32)
    pool_ids = lax.broadcasted_iota(jnp.int32, (blocks, pooled.shape[0]), 1)
    source_hot = (source[:, None] == pool_ids).astype(F32)
    mover = jnp.dot(target_hot, source_hot, preferred_element_type=F32).astype(BF16)
    update = jnp.einsum("qs,srb->qrb", mover, pooled, preferred_element_type=F32).astype(BF16)
    return (moved, update)


def solution(mesh):
    n_dp, n_mp = mesh.shape["dp"], mesh.shape["mp"]

    def on_device(inputs_blk, *rest):
        rows = inputs_blk.shape[2] // n_dp
        if n_mp == 2 and n_dp % PLANE == 0 and rows % 16 == 0 and inputs_blk.shape[1] == 2:
            return fused(n_dp, inputs_blk, *rest)
        return general(inputs_blk, *rest)

    placed = (
        P("dp", "mp", None),
        P("dp", "mp", None),
        P(),
        P(),
        P("mp", "dp", None),
        P("mp", None, None),
        P("mp", "dp", None),
    )
    return jax.shard_map(
        on_device,
        mesh=mesh,
        in_specs=placed,
        out_specs=(P("mp", "dp", None), P("mp", "dp", None)),
        check_vma=False,
    )
```

```python
import functools

import jax
import jax.numpy as jnp
from jax import lax
from jax.experimental import pallas as pl
from jax.experimental.pallas import tpu as pltpu
from jax.sharding import PartitionSpec as P

BETA = 0.9
EPS = 1e-06
PLANE = 4
PARTS = 2
MESH = pl.DeviceIdType.MESH
F32 = jnp.float32
BF16 = jnp.bfloat16


def slots_of(owners):
    block_ids = jnp.arange(owners.shape[0], dtype=jnp.int32)
    same = (owners[None, :] == owners[:, None]) & (block_ids[None, :] < block_ids[:, None])
    return jnp.sum(same.astype(jnp.int32), axis=1)


def scalar_places(ref, blocks, capacity):
    owners = [ref[k] for k in range(blocks)]
    places = []
    for k in range(blocks):
        count = owners[k] * capacity
        for j in range(k):
            count = count + jnp.where(owners[j] == owners[k], 1, 0)
        places.append(count)
    return places


def hot(a, b):
    return jnp.where(a == b, 1.0, 0.0).astype(F32)


def kernel(
    dims,
    x_ref, y_ref, assign_ref, owner_ref, left_hbm, right_hbm, mom_hbm,
    mom_out, upd_out,
    xr_ref, yr_ref, g_ref, r1_ref, t_ref, r2_ref, own_ref, right_ref, left_ref, mom_ref,
    rsel_ref, lband_ref, msel_ref, hb_ref, hall_ref, hfull_ref, bo_ref, both_ref, p_ref, pr_ref, sum_ref,
    local_sem, pre_send, pre_recv, x_send, x_recv, y_send, y_recv, s1_send, s1_recv, s2_send, s2_recv,
    left_send, left_recv, half_send, half_recv, both_send, both_recv, fw_send, fw_recv,
    p_send, p_recv, sum_send, sum_recv,
):
    n_dp, mine, blocks, capacity, size = dims
    lines = n_dp // PLANE
    rows = size // n_dp
    band = size // PLANE
    wing = size // 2
    width = size // PARTS
    me = lax.axis_index("dp")
    core = lax.axis_index("mp")
    q = lax.rem(me, PLANE)
    z = me // PLANE
    x_at, y_at = lax.rem(q, 2), q // 2
    other = 1 - core
    x_mate = (z * PLANE + y_at * 2 + (1 - x_at), core)
    y_mate = (z * PLANE + (1 - y_at) * 2 + x_at, core)
    core_mate = (me, other)

    def plane_mate(j):
        return (z * PLANE + lax.rem(q + j, PLANE), core)

    routes = [
        (x_at, y_at, x_mate, y_mate) if k % 2 == 0 else (y_at, x_at, y_mate, x_mate) for k in range(mine)
    ]

    def at_line(j):
        return (lax.rem(z + j, lines) * PLANE + q, core)

    barrier = pltpu.get_barrier_semaphore()
    partners = [x_mate, y_mate, core_mate] + [at_line(j) for j in range(1, lines)]
    for device in partners:
        pl.semaphore_signal(barrier, inc=1, device_id=device, device_id_type=MESH)

    own = pl.ds(core * capacity, capacity)
    theirs = pl.ds(other * capacity, capacity)
    stored = ((right_hbm, right_ref), (left_hbm, left_ref), (mom_hbm, mom_ref))
    local = [
        pltpu.make_async_copy(src, dst.at[own], local_sem.at[i]) for i, (src, dst) in enumerate(stored)
    ]
    for copy in local:
        copy.start()

    sends = []

    def remote(src, dst, send, recv, device):
        return pltpu.make_async_remote_copy(
            src_ref=src, dst_ref=dst, send_sem=send, recv_sem=recv, device_id=device, device_id_type=MESH
        )

    def start(copy):
        copy.start()
        sends.append(copy)

    def outer(x, y):
        return lax.dot_general(x, y, (((0,), (0,)), ((), ())), preferred_element_type=F32)

    def cols(h):
        return slice(h * width, (h + 1) * width)

    def wing_of(k, a):
        return pl.ds(pl.multiple_of(k * size + a * wing, wing), wing)

    def x_copy(k):
        a, _, mate, _ = routes[k]
        return remote(x_ref.at[:, wing_of(k, 1 - a)], xr_ref.at[k], x_send.at[k], x_recv.at[k], mate)

    def y_copy(k, h):
        src = y_ref.at[:, pl.ds(k * size + h * width, width)]
        return remote(src, yr_ref.at[k, :, pl.ds(h * width, width)], y_send.at[k, h], y_recv.at[k, h], routes[k][2])

    def wing_copy(k, h):
        _, b, _, mate = routes[k]
        src = g_ref.at[k, pl.ds((1 - b) * band, band), pl.ds(h * width, width)]
        return remote(src, r1_ref.at[k, :, pl.ds(h * width, width)], s1_send.at[k, h], s1_recv.at[k, h], mate)

    def line_copy(k, h, j):
        src = t_ref.at[k, pl.ds(lax.rem(z + j, lines) * rows, rows), pl.ds(h * width, width)]
        dst = r2_ref.at[k, j - 1, :, pl.ds(h * width, width)]
        return remote(src, dst, s2_send.at[k, h, j - 1], s2_recv.at[k, h, j - 1], at_line(j))

    def s1(k, h):
        if h == 0:
            x_copy(k).wait_recv()
        y_copy(k, h).wait_recv()
        g_ref[k, :, cols(h)] = g_ref[k, :, cols(h)] + outer(xr_ref[k], yr_ref[k, :, cols(h)])
        start(wing_copy(k, h))
        if h + 1 < PARTS:
            start(y_copy(k, h + 1))

    def s2(k, h):
        b = routes[k][1]
        wing_copy(k, h).wait_recv()
        t_ref[k, :, cols(h)] = g_ref[k, pl.ds(b * band, band), cols(h)] + r1_ref[k, :, cols(h)]
        for j in range(1, lines):
            start(line_copy(k, h, j))

    def s3(k, h):
        total = t_ref[k, pl.ds(z * rows, rows), cols(h)]
        for j in range(1, lines):
            line_copy(k, h, j).wait_recv()
            total = total + r2_ref[k, j - 1, :, cols(h)]
        own_ref[k, :, cols(h)] = total.astype(BF16)

    pl.semaphore_wait(barrier, len(partners))
    for k in range(mine):
        start(x_copy(k))
    for k in range(mine):
        start(y_copy(k, 0))
    for i, (src, dst) in enumerate(stored):
        start(remote(src, dst.at[own], pre_send.at[i], pre_recv.at[i], core_mate))
    for k in range(mine):
        g_ref[k] = outer(x_ref[:, wing_of(k, routes[k][0])], y_ref[:, k * size:(k + 1) * size])

    index = scalar_places(assign_ref, blocks, capacity)
    target = scalar_places(owner_ref, blocks, capacity)
    slots = 2 * capacity

    local_index = [jnp.where(core == 0, index[k], index[mine + k]) for k in range(mine)]

    def select():
        for copy in local:
            copy.wait()
        for i, (src, dst) in enumerate(stored):
            remote(src, dst.at[theirs], pre_send.at[i], pre_recv.at[i], core_mate).wait_recv()
        for k in range(mine):
            picks = [hot(local_index[k], s) for s in range(slots)]

            def pick(at, _, k=k, picks=picks):
                part = pl.ds(pl.multiple_of(at * 64, 64), 64)
                chosen = right_ref[0, part, :].astype(F32) * picks[0]
                for s in range(1, slots):
                    chosen = chosen + right_ref[s, part, :].astype(F32) * picks[s]
                rsel_ref[k, part, :] = chosen.astype(BF16)
                return 0

            lax.fori_loop(0, size // 64, pick, 0)
            chosen = left_ref[0].astype(F32) * picks[0]
            for s in range(1, slots):
                chosen = chosen + left_ref[s].astype(F32) * picks[s]
            lband_ref[q, k] = chosen.astype(BF16)
        for k in range(blocks):
            moment = mom_ref[0] * hot(index[k], 0)
            for s in range(1, slots):
                moment = moment + mom_ref[s] * hot(index[k], s)
            msel_ref[k] = moment

    def left_copy(j, place):
        part = lband_ref.at[place]
        return remote(part, part, left_send.at[j - 1], left_recv.at[j - 1], plane_mate(j))

    def half_copy(j, place):
        device = lax.rem(me + j, n_dp)
        src = hb_ref.at[lax.rem(device, PLANE)]
        return remote(src, hall_ref.at[place], half_send.at[j - 1], half_recv.at[j - 1], (device, core))

    def both_copy(j, place):
        src = bo_ref.at[lax.rem(q + j, PLANE)]
        return remote(src, both_ref.at[core, place], both_send.at[j - 1], both_recv.at[j - 1], plane_mate(j))

    def core_copy(j, at):
        part = both_ref.at[at, lax.rem(q + PLANE - j, PLANE)]
        return remote(part, part, fw_send.at[j], fw_recv.at[j], core_mate)

    def p_copy(j):
        device = (lax.rem(me + j, n_dp), core)
        return remote(p_ref, pr_ref.at[j - 1], p_send.at[j - 1], p_recv.at[j - 1], device)

    def lanes(value):
        partial = value[:, 0:128]
        for at in range(128, value.shape[1], 128):
            partial = partial + value[:, at:at + 128]
        return jnp.sum(partial, axis=0, keepdims=True)

    for step in range(PARTS + 0):
        if step < PARTS:
            for k in range(mine):
                s1(k, step)
        if step >= 0:
            for k in range(mine):
                s2(k, step - 0)
        if step == 1:
            select()
    for j in range(1, PLANE):
        left_copy(j, q).start()
    for h in range(PARTS):
        for k in range(mine):
            s3(k, h)

    p_ref[...] = jnp.zeros_like(p_ref)
    for k in range(mine):
        half = jnp.dot(own_ref[k], rsel_ref[k], preferred_element_type=F32).astype(BF16)
        for j in range(PLANE):
            hb_ref[j, k] = half[:, j * band:(j + 1) * band]
    for j in range(1, n_dp):
        half_copy(j, me).start()
    hall_ref[me] = hb_ref[q]
    for k in range(mine):
        value = own_ref[k].astype(F32)
        p_ref[mine + k:mine + k + 1, :] = lanes(value * value)
    for j in range(1, PLANE):
        left_copy(j, lax.rem(q + PLANE - j, PLANE)).wait_recv()
    for j in range(1, n_dp):
        half_copy(j, lax.rem(me + n_dp - j, n_dp)).wait_recv()
    for device in range(n_dp):
        line, corner = divmod(device, PLANE)
        for k in range(mine):
            a, b = (corner % 2, corner // 2) if k % 2 == 0 else (corner // 2, corner % 2)
            first = (a * 2 + b) * band + line * rows
            hfull_ref[k, first:first + rows, :] = hall_ref[device, k]
    for k in range(mine):
        square = jnp.zeros((1, 128), F32)
        for j in range(PLANE):
            value = jnp.dot(lband_ref[j, k], hfull_ref[k], preferred_element_type=F32)
            bo_ref[j, k] = value
            square = square + lanes(value * value)
        p_ref[k:k + 1, :] = square
    for j in range(1, n_dp):
        p_copy(j).start()
    for j in range(1, PLANE):
        both_copy(j, q).start()
    both_ref[core, q] = bo_ref[q]
    core_copy(0, core).start()
    for j in range(1, PLANE):
        both_copy(j, lax.rem(q + PLANE - j, PLANE)).wait_recv()
        core_copy(j, core).start()
    total = p_ref[...]
    for j in range(1, n_dp):
        p_copy(j).wait_recv()
        total = total + pr_ref[j - 1]
    sum_ref[core] = total
    sum_mine, sum_theirs = sum_ref.at[core], sum_ref.at[other]
    remote(sum_mine, sum_mine, sum_send.at[0], sum_recv.at[0], core_mate).start()
    for j in range(PLANE):
        core_copy(j, other).wait_recv()
    remote(sum_theirs, sum_theirs, sum_send.at[0], sum_recv.at[0], core_mate).wait_recv()

    factors = []
    for k in range(blocks):
        sums = jnp.sum(sum_ref[k // mine], axis=1, keepdims=True)
        at = k % mine
        factors.append(jnp.sqrt(sums[mine + at:mine + at + 1] / (sums[at:at + 1] + EPS)))
    for j in range(PLANE):
        part = slice(j * band, (j + 1) * band)
        grafted = [both_ref[k // mine, j, k % mine] * factors[k] for k in range(blocks)]
        moved = [(BETA * msel_ref[k, :, part] + grafted[k]).astype(BF16).astype(F32) for k in range(blocks)]
        for s in range(capacity):
            here = core * capacity + s
            value = BETA * mom_ref[here, :, part]
            update = jnp.zeros((rows, band), F32)
            for k in range(blocks):
                value = value + grafted[k] * hot(index[k], here)
                update = update + moved[k] * hot(target[k], here)
            mom_out[s, :, part] = value
            upd_out[s, :, part] = update.astype(BF16)
    for j in range(1, PLANE):
        left_copy(j, q).wait_send()
        both_copy(j, q).wait_send()
    for j in range(1, n_dp):
        half_copy(j, me).wait_send()
        p_copy(j).wait_send()
    for j in range(PLANE):
        core_copy(j, core).wait_send()
    remote(sum_mine, sum_mine, sum_send.at[0], sum_recv.at[0], core_mate).wait_send()
    for copy in sends:
        copy.wait_send()


def fused(n_dp, inputs_blk, grads_out, assign, param_owner, left_root, right_root, momentum):
    tokens, mine, size = inputs_blk.shape
    capacity = right_root.shape[0]
    blocks = assign.shape[0]
    rows = size // n_dp
    band, wing, lines = size // PLANE, size // 2, n_dp // PLANE
    slots = 2 * capacity
    vmem = pl.BlockSpec(memory_space=pltpu.VMEM)
    smem = pl.BlockSpec(memory_space=pltpu.SMEM)
    anyw = pl.BlockSpec(memory_space=pl.ANY)
    dma = pltpu.SemaphoreType.DMA
    flops = 2 * mine * tokens * size * size + 2 * blocks * size**3
    return pl.pallas_call(
        functools.partial(kernel, (n_dp, mine, blocks, capacity, size)),
        out_shape=(
            jax.ShapeDtypeStruct((capacity, rows, size), F32),
            jax.ShapeDtypeStruct((capacity, rows, size), BF16),
        ),
        in_specs=[vmem, vmem, smem, smem, anyw, anyw, anyw],
        out_specs=(vmem, vmem),
        scratch_shapes=[
            pltpu.VMEM((mine, tokens, wing), BF16),
            pltpu.VMEM((mine, tokens, size), BF16),
            pltpu.VMEM((mine, wing, size), F32),
            pltpu.VMEM((mine, band, size), F32),
            pltpu.VMEM((mine, band, size), F32),
            pltpu.VMEM((mine, lines - 1, rows, size), F32),
            pltpu.VMEM((mine, rows, size), BF16),
            pltpu.VMEM((slots, size, size), BF16),
            pltpu.VMEM((slots, rows, size), BF16),
            pltpu.VMEM((slots, rows, size), F32),
            pltpu.VMEM((mine, size, size), BF16),
            pltpu.VMEM((PLANE, mine, rows, size), BF16),
            pltpu.VMEM((blocks, rows, size), F32),
            pltpu.VMEM((PLANE, mine, rows, band), BF16),
            pltpu.VMEM((n_dp, mine, rows, band), BF16),
            pltpu.VMEM((mine, size, band), BF16),
            pltpu.VMEM((PLANE, mine, rows, band), F32),
            pltpu.VMEM((2, PLANE, mine, rows, band), F32),
            pltpu.VMEM((8, 128), F32),
            pltpu.VMEM((n_dp - 1, 8, 128), F32),
            pltpu.VMEM((2, 8, 128), F32),
            dma((3,)), dma((3,)), dma((3,)),
            dma((mine,)), dma((mine,)),
            dma((mine, PARTS)), dma((mine, PARTS)),
            dma((mine, PARTS)), dma((mine, PARTS)),
            dma((mine, PARTS, lines - 1)), dma((mine, PARTS, lines - 1)),
            dma((PLANE - 1,)), dma((PLANE - 1,)),
            dma((n_dp - 1,)), dma((n_dp - 1,)),
            dma((PLANE - 1,)), dma((PLANE - 1,)),
            dma((PLANE,)), dma((PLANE,)),
            dma((n_dp - 1,)), dma((n_dp - 1,)),
            dma((1,)), dma((1,)),
        ],
        compiler_params=pltpu.CompilerParams(
            collective_id=0, has_side_effects=True, vmem_limit_bytes=40 * 1024 * 1024
        ),
        cost_estimate=pl.CostEstimate(flops=flops, bytes_accessed=4 * 1024 * 1024, transcendentals=0),
    )(
        inputs_blk.reshape(tokens, mine * size),
        grads_out.reshape(tokens, mine * size),
        assign, param_owner, left_root, right_root, momentum,
    )


def general(inputs_blk, grads_out, assign, param_owner, left_root, right_root, momentum):
    capacity = right_root.shape[0]
    blocks = assign.shape[0]
    my_index = lax.axis_index("mp")
    reduced = lax.psum_scatter(
        jnp.einsum("tkr,tkc->rkc", inputs_blk, grads_out, preferred_element_type=F32),
        "dp",
        scatter_dimension=0,
        tiled=True,
    )
    rounded = reduced.astype(BF16)
    gathered = lax.all_gather(rounded, "mp", axis=1, tiled=True)
    slot = slots_of(assign)
    slot_ids = lax.broadcasted_iota(jnp.int32, (capacity, blocks), 0)
    chooser = ((assign[None, :] == my_index) & (slot[None, :] == slot_ids)).astype(BF16)
    owned = jnp.einsum("ck,rkb->crb", chooser, gathered, preferred_element_type=F32).astype(BF16)
    half = jnp.einsum("crb,cbe->cre", owned, right_root, preferred_element_type=F32).astype(BF16)
    both = jnp.einsum(
        "cri,cie->cre",
        left_root,
        lax.all_gather(half, "dp", axis=1, tiled=True),
        preferred_element_type=F32,
    )
    grad_square = jnp.sum(jnp.square(owned.astype(F32)), axis=(1, 2))
    prec_square = jnp.sum(both * both, axis=(1, 2))
    grad_square, prec_square = lax.psum((grad_square, prec_square), "dp")
    factor = jnp.sqrt(grad_square / (prec_square + EPS))
    moved = BETA * momentum + both * factor[:, None, None]
    sending = moved.astype(BF16)
    pooled = lax.all_gather(sending, "mp", axis=0, tiled=True)
    place = slots_of(param_owner)
    source = assign * capacity + slot
    target_hot = ((param_owner[None, :] == my_index) & (place[None, :] == slot_ids)).astype(F32)
    pool_ids = lax.broadcasted_iota(jnp.int32, (blocks, pooled.shape[0]), 1)
    source_hot = (source[:, None] == pool_ids).astype(F32)
    mover = jnp.dot(target_hot, source_hot, preferred_element_type=F32).astype(BF16)
    update = jnp.einsum("qs,srb->qrb", mover, pooled, preferred_element_type=F32).astype(BF16)
    return (moved, update)


def solution(mesh):
    n_dp, n_mp = mesh.shape["dp"], mesh.shape["mp"]

    def on_device(inputs_blk, *rest):
        rows = inputs_blk.shape[2] // n_dp
        if n_mp == 2 and n_dp % PLANE == 0 and rows % 16 == 0 and inputs_blk.shape[1] == 2:
            return fused(n_dp, inputs_blk, *rest)
        return general(inputs_blk, *rest)

    placed = (
        P("dp", "mp", None),
        P("dp", "mp", None),
        P(),
        P(),
        P("mp", "dp", None),
        P("mp", None, None),
        P("mp", "dp", None),
    )
    return jax.shard_map(
        on_device,
        mesh=mesh,
        in_specs=placed,
        out_specs=(P("mp", "dp", None), P("mp", "dp", None)),
        check_vma=False,
    )
```

```python
import functools

import jax
import jax.numpy as jnp
from jax import lax
from jax.experimental import pallas as pl
from jax.experimental.pallas import tpu as pltpu
from jax.sharding import PartitionSpec as P

BETA = 0.9
EPS = 1e-06
PLANE = 4
PARTS = 2
MESH = pl.DeviceIdType.MESH
F32 = jnp.float32
BF16 = jnp.bfloat16


def slots_of(owners):
    block_ids = jnp.arange(owners.shape[0], dtype=jnp.int32)
    same = (owners[None, :] == owners[:, None]) & (block_ids[None, :] < block_ids[:, None])
    return jnp.sum(same.astype(jnp.int32), axis=1)


def scalar_places(ref, blocks, capacity):
    owners = [ref[k] for k in range(blocks)]
    places = []
    for k in range(blocks):
        count = owners[k] * capacity
        for j in range(k):
            count = count + jnp.where(owners[j] == owners[k], 1, 0)
        places.append(count)
    return places


def hot(a, b):
    return jnp.where(a == b, 1.0, 0.0).astype(F32)


def kernel(
    dims,
    x_ref, y_ref, assign_ref, owner_ref, left_hbm, right_hbm, mom_hbm,
    mom_out, upd_out,
    xr_ref, yr_ref, g_ref, r1_ref, t_ref, r2_ref, own_ref, right_ref, left_ref, mom_ref,
    rsel_ref, lband_ref, msel_ref, hb_ref, hall_ref, hfull_ref, bo_ref, both_ref, p_ref, pr_ref, sum_ref,
    local_sem, pre_send, pre_recv, x_send, x_recv, y_send, y_recv, s1_send, s1_recv, s2_send, s2_recv,
    left_send, left_recv, half_send, half_recv, both_send, both_recv, fw_send, fw_recv,
    p_send, p_recv, sum_send, sum_recv,
    gz_ref, rz_ref, tz_ref, uz_ref, gz_send, gz_recv, tz_send, tz_recv,
):
    n_dp, mine, blocks, capacity, size = dims
    lines = n_dp // PLANE
    rows = size // n_dp
    band = size // PLANE
    wing = size // 2
    tail = size // 4
    starts, widths = (0, size // 4), (size // 4, size // 2)
    me = lax.axis_index("dp")
    core = lax.axis_index("mp")
    q = lax.rem(me, PLANE)
    z = me // PLANE
    x_at, y_at = lax.rem(q, 2), q // 2
    other = 1 - core
    x_mate = (z * PLANE + y_at * 2 + (1 - x_at), core)
    y_mate = (z * PLANE + (1 - y_at) * 2 + x_at, core)
    core_mate = (me, other)

    def plane_mate(j):
        return (z * PLANE + lax.rem(q + j, PLANE), core)

    routes = [
        (x_at, y_at, x_mate, y_mate) if k % 2 == 0 else (y_at, x_at, y_mate, x_mate) for k in range(mine)
    ]

    def at_line(j):
        return (lax.rem(z + j, lines) * PLANE + q, core)

    barrier = pltpu.get_barrier_semaphore()
    partners = [x_mate, y_mate, core_mate] + [at_line(j) for j in range(1, lines)]
    for device in partners:
        pl.semaphore_signal(barrier, inc=1, device_id=device, device_id_type=MESH)

    own = pl.ds(core * capacity, capacity)
    theirs = pl.ds(other * capacity, capacity)
    stored = ((right_hbm, right_ref), (left_hbm, left_ref), (mom_hbm, mom_ref))
    local = [
        pltpu.make_async_copy(src, dst.at[own], local_sem.at[i]) for i, (src, dst) in enumerate(stored)
    ]
    for copy in local:
        copy.start()

    sends = []

    def remote(src, dst, send, recv, device):
        return pltpu.make_async_remote_copy(
            src_ref=src, dst_ref=dst, send_sem=send, recv_sem=recv, device_id=device, device_id_type=MESH
        )

    def start(copy):
        copy.start()
        sends.append(copy)

    def outer(x, y):
        return lax.dot_general(x, y, (((0,), (0,)), ((), ())), preferred_element_type=F32)

    def cols(h):
        return slice(starts[h], starts[h] + widths[h])

    def wing_of(k, a):
        return pl.ds(pl.multiple_of(k * size + a * wing, wing), wing)

    def x_copy(k):
        a, _, mate, _ = routes[k]
        return remote(x_ref.at[:, wing_of(k, 1 - a)], xr_ref.at[k], x_send.at[k], x_recv.at[k], mate)

    def y_copy(k, h):
        src = y_ref.at[:, pl.ds(k * size + starts[h], widths[h])]
        return remote(src, yr_ref.at[k, :, pl.ds(starts[h], widths[h])], y_send.at[k, h], y_recv.at[k, h], routes[k][2])

    def wing_copy(k, h):
        _, b, _, mate = routes[k]
        src = g_ref.at[k, pl.ds((1 - b) * band, band), pl.ds(starts[h], widths[h])]
        return remote(src, r1_ref.at[k, :, pl.ds(starts[h], widths[h])], s1_send.at[k, h], s1_recv.at[k, h], mate)

    def line_copy(k, h, j):
        src = t_ref.at[k, pl.ds(lax.rem(z + j, lines) * rows, rows), pl.ds(starts[h], widths[h])]
        dst = r2_ref.at[k, j - 1, :, pl.ds(starts[h], widths[h])]
        return remote(src, dst, s2_send.at[k, h, j - 1], s2_recv.at[k, h, j - 1], at_line(j))

    def s1(k, h):
        if h == 0:
            x_copy(k).wait_recv()
        y_copy(k, h).wait_recv()
        g_ref[k, :, cols(h)] = g_ref[k, :, cols(h)] + outer(xr_ref[k], yr_ref[k, :, cols(h)])
        start(wing_copy(k, h))
        if h + 1 < PARTS:
            start(y_copy(k, h + 1))

    def s2(k, h):
        b = routes[k][1]
        wing_copy(k, h).wait_recv()
        t_ref[k, :, cols(h)] = g_ref[k, pl.ds(b * band, band), cols(h)] + r1_ref[k, :, cols(h)]
        for j in range(1, lines):
            start(line_copy(k, h, j))

    def s3(k, h):
        total = t_ref[k, pl.ds(z * rows, rows), cols(h)]
        for j in range(1, lines):
            line_copy(k, h, j).wait_recv()
            total = total + r2_ref[k, j - 1, :, cols(h)]
        own_ref[k, :, cols(h)] = total.astype(BF16)

    def corner_band(k, corner):
        return corner % 2 * 2 + corner // 2 if k % 2 == 0 else corner

    def gz_copy(j):
        place = lax.rem(z + j, lines)
        return remote(gz_ref.at[place], rz_ref.at[j - 1], gz_send.at[j - 1], gz_recv.at[j - 1], at_line(j))

    def tz_copy(j):
        place = lax.rem(q + j, PLANE)
        return remote(tz_ref.at[place], uz_ref.at[j - 1], tz_send.at[j - 1], tz_recv.at[j - 1], plane_mate(j))

    for k in range(mine):
        value = outer(x_ref[:, k * size:(k + 1) * size], y_ref[:, (k + 1) * size - tail:(k + 1) * size])
        for at in range(PLANE):
            for line in range(lines):
                first = at * band + line * rows
                gz_ref[line, k, at] = value[first:first + rows]
    pl.semaphore_wait(barrier, len(partners))
    for k in range(mine):
        start(x_copy(k))
    for k in range(mine):
        start(y_copy(k, 0))
    for j in range(1, lines):
        start(gz_copy(j))
    for i, (src, dst) in enumerate(stored):
        start(remote(src, dst.at[own], pre_send.at[i], pre_recv.at[i], core_mate))
    for k in range(mine):
        g_ref[k] = outer(x_ref[:, wing_of(k, routes[k][0])], y_ref[:, k * size:(k + 1) * size - tail])

    index = scalar_places(assign_ref, blocks, capacity)
    target = scalar_places(owner_ref, blocks, capacity)
    slots = 2 * capacity

    local_index = [jnp.where(core == 0, index[k], index[mine + k]) for k in range(mine)]

    def select():
        for copy in local:
            copy.wait()
        for i, (src, dst) in enumerate(stored):
            remote(src, dst.at[theirs], pre_send.at[i], pre_recv.at[i], core_mate).wait_recv()
        for k in range(mine):
            picks = [hot(local_index[k], s) for s in range(slots)]

            def pick(at, _, k=k, picks=picks):
                part = pl.ds(pl.multiple_of(at * 64, 64), 64)
                chosen = right_ref[0, part, :].astype(F32) * picks[0]
                for s in range(1, slots):
                    chosen = chosen + right_ref[s, part, :].astype(F32) * picks[s]
                rsel_ref[k, part, :] = chosen.astype(BF16)
                return 0

            lax.fori_loop(0, size // 64, pick, 0)
            chosen = left_ref[0].astype(F32) * picks[0]
            for s in range(1, slots):
                chosen = chosen + left_ref[s].astype(F32) * picks[s]
            lband_ref[q, k] = chosen.astype(BF16)
        for k in range(blocks):
            moment = mom_ref[0] * hot(index[k], 0)
            for s in range(1, slots):
                moment = moment + mom_ref[s] * hot(index[k], s)
            msel_ref[k] = moment

    def left_copy(j, place):
        part = lband_ref.at[place]
        return remote(part, part, left_send.at[j - 1], left_recv.at[j - 1], plane_mate(j))

    def half_copy(j, place):
        device = lax.rem(me + j, n_dp)
        src = hb_ref.at[lax.rem(device, PLANE)]
        return remote(src, hall_ref.at[place], half_send.at[j - 1], half_recv.at[j - 1], (device, core))

    def both_copy(j, place):
        src = bo_ref.at[lax.rem(q + j, PLANE)]
        return remote(src, both_ref.at[core, place], both_send.at[j - 1], both_recv.at[j - 1], plane_mate(j))

    def core_copy(j, at):
        part = both_ref.at[at, lax.rem(q + PLANE - j, PLANE)]
        return remote(part, part, fw_send.at[j], fw_recv.at[j], core_mate)

    def p_copy(j):
        device = (lax.rem(me + j, n_dp), core)
        return remote(p_ref, pr_ref.at[j - 1], p_send.at[j - 1], p_recv.at[j - 1], device)

    def lanes(value):
        partial = value[:, 0:128]
        for at in range(128, value.shape[1], 128):
            partial = partial + value[:, at:at + 128]
        return jnp.sum(partial, axis=0, keepdims=True)

    for step in range(PARTS + 0):
        if step < PARTS:
            for k in range(mine):
                s1(k, step)
        if step >= 0:
            for k in range(mine):
                s2(k, step - 0)
        if step == 1:
            select()
    for j in range(1, lines):
        gz_copy(j).wait_recv()
    for corner in range(PLANE):
        for k in range(mine):
            at = corner_band(k, corner)
            total = gz_ref[z, k, at]
            for j in range(1, lines):
                total = total + rz_ref[j - 1, k, at]
            tz_ref[corner, k] = total
    for j in range(1, PLANE):
        start(tz_copy(j))
    for j in range(1, PLANE):
        left_copy(j, q).start()
    for h in range(PARTS):
        for k in range(mine):
            s3(k, h)
    for j in range(1, PLANE):
        tz_copy(j).wait_recv()
    for k in range(mine):
        total = tz_ref[q, k]
        for j in range(1, PLANE):
            total = total + uz_ref[j - 1, k]
        own_ref[k, :, size - tail:size] = total.astype(BF16)

    p_ref[...] = jnp.zeros_like(p_ref)
    for k in range(mine):
        half = jnp.dot(own_ref[k], rsel_ref[k], preferred_element_type=F32).astype(BF16)
        for j in range(PLANE):
            hb_ref[j, k] = half[:, j * band:(j + 1) * band]
    for j in range(1, n_dp):
        half_copy(j, me).start()
    hall_ref[me] = hb_ref[q]
    for k in range(mine):
        value = own_ref[k].astype(F32)
        p_ref[mine + k:mine + k + 1, :] = lanes(value * value)
    for j in range(1, PLANE):
        left_copy(j, lax.rem(q + PLANE - j, PLANE)).wait_recv()
    for j in range(1, n_dp):
        half_copy(j, lax.rem(me + n_dp - j, n_dp)).wait_recv()
    for device in range(n_dp):
        line, corner = divmod(device, PLANE)
        for k in range(mine):
            a, b = (corner % 2, corner // 2) if k % 2 == 0 else (corner // 2, corner % 2)
            first = (a * 2 + b) * band + line * rows
            hfull_ref[k, first:first + rows, :] = hall_ref[device, k]
    for k in range(mine):
        square = jnp.zeros((1, 128), F32)
        for j in range(PLANE):
            value = jnp.dot(lband_ref[j, k], hfull_ref[k], preferred_element_type=F32)
            bo_ref[j, k] = value
            square = square + lanes(value * value)
        p_ref[k:k + 1, :] = square
    for j in range(1, n_dp):
        p_copy(j).start()
    for j in range(1, PLANE):
        both_copy(j, q).start()
    both_ref[core, q] = bo_ref[q]
    core_copy(0, core).start()
    for j in range(1, PLANE):
        both_copy(j, lax.rem(q + PLANE - j, PLANE)).wait_recv()
        core_copy(j, core).start()
    total = p_ref[...]
    for j in range(1, n_dp):
        p_copy(j).wait_recv()
        total = total + pr_ref[j - 1]
    sum_ref[core] = total
    sum_mine, sum_theirs = sum_ref.at[core], sum_ref.at[other]
    remote(sum_mine, sum_mine, sum_send.at[0], sum_recv.at[0], core_mate).start()
    for j in range(PLANE):
        core_copy(j, other).wait_recv()
    remote(sum_theirs, sum_theirs, sum_send.at[0], sum_recv.at[0], core_mate).wait_recv()

    factors = []
    for k in range(blocks):
        sums = jnp.sum(sum_ref[k // mine], axis=1, keepdims=True)
        at = k % mine
        factors.append(jnp.sqrt(sums[mine + at:mine + at + 1] / (sums[at:at + 1] + EPS)))
    for j in range(PLANE):
        part = slice(j * band, (j + 1) * band)
        grafted = [both_ref[k // mine, j, k % mine] * factors[k] for k in range(blocks)]
        moved = [(BETA * msel_ref[k, :, part] + grafted[k]).astype(BF16).astype(F32) for k in range(blocks)]
        for s in range(capacity):
            here = core * capacity + s
            value = BETA * mom_ref[here, :, part]
            update = jnp.zeros((rows, band), F32)
            for k in range(blocks):
                value = value + grafted[k] * hot(index[k], here)
                update = update + moved[k] * hot(target[k], here)
            mom_out[s, :, part] = value
            upd_out[s, :, part] = update.astype(BF16)
    for j in range(1, PLANE):
        left_copy(j, q).wait_send()
        both_copy(j, q).wait_send()
    for j in range(1, n_dp):
        half_copy(j, me).wait_send()
        p_copy(j).wait_send()
    for j in range(PLANE):
        core_copy(j, core).wait_send()
    remote(sum_mine, sum_mine, sum_send.at[0], sum_recv.at[0], core_mate).wait_send()
    for copy in sends:
        copy.wait_send()


def fused(n_dp, inputs_blk, grads_out, assign, param_owner, left_root, right_root, momentum):
    tokens, mine, size = inputs_blk.shape
    capacity = right_root.shape[0]
    blocks = assign.shape[0]
    rows = size // n_dp
    band, wing, lines = size // PLANE, size // 2, n_dp // PLANE
    slots = 2 * capacity
    vmem = pl.BlockSpec(memory_space=pltpu.VMEM)
    smem = pl.BlockSpec(memory_space=pltpu.SMEM)
    anyw = pl.BlockSpec(memory_space=pl.ANY)
    dma = pltpu.SemaphoreType.DMA
    flops = 2 * mine * tokens * size * size + 2 * blocks * size**3
    return pl.pallas_call(
        functools.partial(kernel, (n_dp, mine, blocks, capacity, size)),
        out_shape=(
            jax.ShapeDtypeStruct((capacity, rows, size), F32),
            jax.ShapeDtypeStruct((capacity, rows, size), BF16),
        ),
        in_specs=[vmem, vmem, smem, smem, anyw, anyw, anyw],
        out_specs=(vmem, vmem),
        scratch_shapes=[
            pltpu.VMEM((mine, tokens, wing), BF16),
            pltpu.VMEM((mine, tokens, size), BF16),
            pltpu.VMEM((mine, wing, size - size // 4), F32),
            pltpu.VMEM((mine, band, size), F32),
            pltpu.VMEM((mine, band, size), F32),
            pltpu.VMEM((mine, lines - 1, rows, size), F32),
            pltpu.VMEM((mine, rows, size), BF16),
            pltpu.VMEM((slots, size, size), BF16),
            pltpu.VMEM((slots, rows, size), BF16),
            pltpu.VMEM((slots, rows, size), F32),
            pltpu.VMEM((mine, size, size), BF16),
            pltpu.VMEM((PLANE, mine, rows, size), BF16),
            pltpu.VMEM((blocks, rows, size), F32),
            pltpu.VMEM((PLANE, mine, rows, band), BF16),
            pltpu.VMEM((n_dp, mine, rows, band), BF16),
            pltpu.VMEM((mine, size, band), BF16),
            pltpu.VMEM((PLANE, mine, rows, band), F32),
            pltpu.VMEM((2, PLANE, mine, rows, band), F32),
            pltpu.VMEM((8, 128), F32),
            pltpu.VMEM((n_dp - 1, 8, 128), F32),
            pltpu.VMEM((2, 8, 128), F32),
            dma((3,)), dma((3,)), dma((3,)),
            dma((mine,)), dma((mine,)),
            dma((mine, PARTS)), dma((mine, PARTS)),
            dma((mine, PARTS)), dma((mine, PARTS)),
            dma((mine, PARTS, lines - 1)), dma((mine, PARTS, lines - 1)),
            dma((PLANE - 1,)), dma((PLANE - 1,)),
            dma((n_dp - 1,)), dma((n_dp - 1,)),
            dma((PLANE - 1,)), dma((PLANE - 1,)),
            dma((PLANE,)), dma((PLANE,)),
            dma((n_dp - 1,)), dma((n_dp - 1,)),
            dma((1,)), dma((1,)),
            pltpu.VMEM((lines, mine, PLANE, rows, size // 4), F32),
            pltpu.VMEM((lines - 1, mine, PLANE, rows, size // 4), F32),
            pltpu.VMEM((PLANE, mine, rows, size // 4), F32),
            pltpu.VMEM((PLANE - 1, mine, rows, size // 4), F32),
            dma((lines - 1,)), dma((lines - 1,)),
            dma((PLANE - 1,)), dma((PLANE - 1,)),
        ],
        compiler_params=pltpu.CompilerParams(
            collective_id=0, has_side_effects=True, vmem_limit_bytes=40 * 1024 * 1024
        ),
        cost_estimate=pl.CostEstimate(flops=flops, bytes_accessed=4 * 1024 * 1024, transcendentals=0),
    )(
        inputs_blk.reshape(tokens, mine * size),
        grads_out.reshape(tokens, mine * size),
        assign, param_owner, left_root, right_root, momentum,
    )


def general(inputs_blk, grads_out, assign, param_owner, left_root, right_root, momentum):
    capacity = right_root.shape[0]
    blocks = assign.shape[0]
    my_index = lax.axis_index("mp")
    reduced = lax.psum_scatter(
        jnp.einsum("tkr,tkc->rkc", inputs_blk, grads_out, preferred_element_type=F32),
        "dp",
        scatter_dimension=0,
        tiled=True,
    )
    rounded = reduced.astype(BF16)
    gathered = lax.all_gather(rounded, "mp", axis=1, tiled=True)
    slot = slots_of(assign)
    slot_ids = lax.broadcasted_iota(jnp.int32, (capacity, blocks), 0)
    chooser = ((assign[None, :] == my_index) & (slot[None, :] == slot_ids)).astype(BF16)
    owned = jnp.einsum("ck,rkb->crb", chooser, gathered, preferred_element_type=F32).astype(BF16)
    half = jnp.einsum("crb,cbe->cre", owned, right_root, preferred_element_type=F32).astype(BF16)
    both = jnp.einsum(
        "cri,cie->cre",
        left_root,
        lax.all_gather(half, "dp", axis=1, tiled=True),
        preferred_element_type=F32,
    )
    grad_square = jnp.sum(jnp.square(owned.astype(F32)), axis=(1, 2))
    prec_square = jnp.sum(both * both, axis=(1, 2))
    grad_square, prec_square = lax.psum((grad_square, prec_square), "dp")
    factor = jnp.sqrt(grad_square / (prec_square + EPS))
    moved = BETA * momentum + both * factor[:, None, None]
    sending = moved.astype(BF16)
    pooled = lax.all_gather(sending, "mp", axis=0, tiled=True)
    place = slots_of(param_owner)
    source = assign * capacity + slot
    target_hot = ((param_owner[None, :] == my_index) & (place[None, :] == slot_ids)).astype(F32)
    pool_ids = lax.broadcasted_iota(jnp.int32, (blocks, pooled.shape[0]), 1)
    source_hot = (source[:, None] == pool_ids).astype(F32)
    mover = jnp.dot(target_hot, source_hot, preferred_element_type=F32).astype(BF16)
    update = jnp.einsum("qs,srb->qrb", mover, pooled, preferred_element_type=F32).astype(BF16)
    return (moved, update)


def solution(mesh):
    n_dp, n_mp = mesh.shape["dp"], mesh.shape["mp"]

    def on_device(inputs_blk, *rest):
        rows = inputs_blk.shape[2] // n_dp
        if n_mp == 2 and n_dp % PLANE == 0 and rows % 16 == 0 and inputs_blk.shape[1] == 2:
            return fused(n_dp, inputs_blk, *rest)
        return general(inputs_blk, *rest)

    placed = (
        P("dp", "mp", None),
        P("dp", "mp", None),
        P(),
        P(),
        P("mp", "dp", None),
        P("mp", None, None),
        P("mp", "dp", None),
    )
    return jax.shard_map(
        on_device,
        mesh=mesh,
        in_specs=placed,
        out_specs=(P("mp", "dp", None), P("mp", "dp", None)),
        check_vma=False,
    )
```

```python
import functools

import jax
import jax.numpy as jnp
from jax import lax
from jax.experimental import pallas as pl
from jax.experimental.pallas import tpu as pltpu
from jax.sharding import PartitionSpec as P

BETA = 0.9
EPS = 1e-06
PLANE = 4
PARTS = 2
MESH = pl.DeviceIdType.MESH
F32 = jnp.float32
BF16 = jnp.bfloat16


def slots_of(owners):
    block_ids = jnp.arange(owners.shape[0], dtype=jnp.int32)
    same = (owners[None, :] == owners[:, None]) & (block_ids[None, :] < block_ids[:, None])
    return jnp.sum(same.astype(jnp.int32), axis=1)


def scalar_places(ref, blocks, capacity):
    owners = [ref[k] for k in range(blocks)]
    places = []
    for k in range(blocks):
        count = owners[k] * capacity
        for j in range(k):
            count = count + jnp.where(owners[j] == owners[k], 1, 0)
        places.append(count)
    return places


def hot(a, b):
    return jnp.where(a == b, 1.0, 0.0).astype(F32)


def kernel(
    dims,
    x_ref, y_ref, assign_ref, owner_ref, left_hbm, right_hbm, mom_hbm,
    mom_out, upd_out,
    xr_ref, yr_ref, g_ref, r1_ref, t_ref, r2_ref, own_ref, right_ref, left_ref, mom_ref,
    rsel_ref, lband_ref, msel_ref, hb_ref, hall_ref, hfull_ref, bo_ref, both_ref, p_ref, pr_ref, sum_ref,
    local_sem, pre_send, pre_recv, x_send, x_recv, y_send, y_recv, s1_send, s1_recv, s2_send, s2_recv,
    left_send, left_recv, half_send, half_recv, both_send, both_recv, fw_send, fw_recv,
    p_send, p_recv, sum_send, sum_recv,
    gz_ref, rz_ref, tz_ref, uz_ref, gz_send, gz_recv, tz_send, tz_recv,
):
    n_dp, mine, blocks, capacity, size = dims
    lines = n_dp // PLANE
    rows = size // n_dp
    band = size // PLANE
    wing = size // 2
    tail = size // 4
    starts, widths = (0, size // 4), (size // 4, size // 2)
    me = lax.axis_index("dp")
    core = lax.axis_index("mp")
    q = lax.rem(me, PLANE)
    z = me // PLANE
    x_at, y_at = lax.rem(q, 2), q // 2
    other = 1 - core
    x_mate = (z * PLANE + y_at * 2 + (1 - x_at), core)
    y_mate = (z * PLANE + (1 - y_at) * 2 + x_at, core)
    core_mate = (me, other)

    def plane_mate(j):
        return (z * PLANE + lax.rem(q + j, PLANE), core)

    routes = [
        (x_at, y_at, x_mate, y_mate) if k % 2 == 0 else (y_at, x_at, y_mate, x_mate) for k in range(mine)
    ]

    def at_line(j):
        return (lax.rem(z + j, lines) * PLANE + q, core)

    barrier = pltpu.get_barrier_semaphore()
    partners = [x_mate, y_mate, core_mate] + [at_line(j) for j in range(1, lines)]
    for device in partners:
        pl.semaphore_signal(barrier, inc=1, device_id=device, device_id_type=MESH)

    own = pl.ds(core * capacity, capacity)
    theirs = pl.ds(other * capacity, capacity)
    stored = ((right_hbm, right_ref), (left_hbm, left_ref), (mom_hbm, mom_ref))
    local = [
        pltpu.make_async_copy(src, dst.at[own], local_sem.at[i]) for i, (src, dst) in enumerate(stored)
    ]
    for copy in local:
        copy.start()

    sends = []

    def remote(src, dst, send, recv, device):
        return pltpu.make_async_remote_copy(
            src_ref=src, dst_ref=dst, send_sem=send, recv_sem=recv, device_id=device, device_id_type=MESH
        )

    def start(copy):
        copy.start()
        sends.append(copy)

    def outer(x, y):
        return lax.dot_general(x, y, (((0,), (0,)), ((), ())), preferred_element_type=F32)

    def cols(h):
        return slice(starts[h], starts[h] + widths[h])

    def wing_of(k, a):
        return pl.ds(pl.multiple_of(k * size + a * wing, wing), wing)

    def x_copy(k):
        a, _, mate, _ = routes[k]
        return remote(x_ref.at[:, wing_of(k, 1 - a)], xr_ref.at[k], x_send.at[k], x_recv.at[k], mate)

    def y_copy(k, h):
        src = y_ref.at[:, pl.ds(k * size + starts[h], widths[h])]
        return remote(src, yr_ref.at[k, :, pl.ds(starts[h], widths[h])], y_send.at[k, h], y_recv.at[k, h], routes[k][2])

    def wing_copy(k, h):
        _, b, _, mate = routes[k]
        src = g_ref.at[k, pl.ds((1 - b) * band, band), pl.ds(starts[h], widths[h])]
        return remote(src, r1_ref.at[k, :, pl.ds(starts[h], widths[h])], s1_send.at[k, h], s1_recv.at[k, h], mate)

    def line_copy(k, h, j):
        src = t_ref.at[k, pl.ds(lax.rem(z + j, lines) * rows, rows), pl.ds(starts[h], widths[h])]
        dst = r2_ref.at[k, j - 1, :, pl.ds(starts[h], widths[h])]
        return remote(src, dst, s2_send.at[k, h, j - 1], s2_recv.at[k, h, j - 1], at_line(j))

    def s1(k, h):
        if h == 0:
            x_copy(k).wait_recv()
        y_copy(k, h).wait_recv()
        g_ref[k, :, cols(h)] = g_ref[k, :, cols(h)] + outer(xr_ref[k], yr_ref[k, :, cols(h)])
        start(wing_copy(k, h))
        if h + 1 < PARTS:
            start(y_copy(k, h + 1))

    def s2(k, h):
        b = routes[k][1]
        wing_copy(k, h).wait_recv()
        t_ref[k, :, cols(h)] = g_ref[k, pl.ds(b * band, band), cols(h)] + r1_ref[k, :, cols(h)]
        for j in range(1, lines):
            start(line_copy(k, h, j))

    def s3(k, h):
        total = t_ref[k, pl.ds(z * rows, rows), cols(h)]
        for j in range(1, lines):
            line_copy(k, h, j).wait_recv()
            total = total + r2_ref[k, j - 1, :, cols(h)]
        own_ref[k, :, cols(h)] = total.astype(BF16)

    def corner_band(k, corner):
        return corner % 2 * 2 + corner // 2 if k % 2 == 0 else corner

    def gz_copy(j):
        place = lax.rem(z + j, lines)
        return remote(gz_ref.at[place], rz_ref.at[j - 1], gz_send.at[j - 1], gz_recv.at[j - 1], at_line(j))

    def tz_copy(j):
        place = lax.rem(q + j, PLANE)
        return remote(tz_ref.at[place], uz_ref.at[j - 1], tz_send.at[j - 1], tz_recv.at[j - 1], plane_mate(j))

    for k in range(mine):
        value = outer(x_ref[:, k * size:(k + 1) * size], y_ref[:, (k + 1) * size - tail:(k + 1) * size])
        for at in range(PLANE):
            for line in range(lines):
                first = at * band + line * rows
                gz_ref[line, k, at] = value[first:first + rows]
    pl.semaphore_wait(barrier, len(partners))
    for j in range(1, lines):
        start(gz_copy(j))
    for k in range(mine):
        start(x_copy(k))
    for k in range(mine):
        start(y_copy(k, 0))
    for i, (src, dst) in enumerate(stored):
        start(remote(src, dst.at[own], pre_send.at[i], pre_recv.at[i], core_mate))
    for k in range(mine):
        g_ref[k] = outer(x_ref[:, wing_of(k, routes[k][0])], y_ref[:, k * size:(k + 1) * size - tail])

    index = scalar_places(assign_ref, blocks, capacity)
    target = scalar_places(owner_ref, blocks, capacity)
    slots = 2 * capacity

    local_index = [jnp.where(core == 0, index[k], index[mine + k]) for k in range(mine)]

    def select():
        for copy in local:
            copy.wait()
        for i, (src, dst) in enumerate(stored):
            remote(src, dst.at[theirs], pre_send.at[i], pre_recv.at[i], core_mate).wait_recv()
        for k in range(mine):
            picks = [hot(local_index[k], s) for s in range(slots)]

            def pick(at, _, k=k, picks=picks):
                part = pl.ds(pl.multiple_of(at * 64, 64), 64)
                chosen = right_ref[0, part, :].astype(F32) * picks[0]
                for s in range(1, slots):
                    chosen = chosen + right_ref[s, part, :].astype(F32) * picks[s]
                rsel_ref[k, part, :] = chosen.astype(BF16)
                return 0

            lax.fori_loop(0, size // 64, pick, 0)
            chosen = left_ref[0].astype(F32) * picks[0]
            for s in range(1, slots):
                chosen = chosen + left_ref[s].astype(F32) * picks[s]
            lband_ref[q, k] = chosen.astype(BF16)
        for k in range(blocks):
            moment = mom_ref[0] * hot(index[k], 0)
            for s in range(1, slots):
                moment = moment + mom_ref[s] * hot(index[k], s)
            msel_ref[k] = moment

    def left_copy(j, place):
        part = lband_ref.at[place]
        return remote(part, part, left_send.at[j - 1], left_recv.at[j - 1], plane_mate(j))

    def half_copy(j, place):
        device = lax.rem(me + j, n_dp)
        src = hb_ref.at[lax.rem(device, PLANE)]
        return remote(src, hall_ref.at[place], half_send.at[j - 1], half_recv.at[j - 1], (device, core))

    def both_copy(j, place):
        src = bo_ref.at[lax.rem(q + j, PLANE)]
        return remote(src, both_ref.at[core, place], both_send.at[j - 1], both_recv.at[j - 1], plane_mate(j))

    def core_copy(j, at):
        part = both_ref.at[at, lax.rem(q + PLANE - j, PLANE)]
        return remote(part, part, fw_send.at[j], fw_recv.at[j], core_mate)

    def p_copy(j):
        device = (lax.rem(me + j, n_dp), core)
        return remote(p_ref, pr_ref.at[j - 1], p_send.at[j - 1], p_recv.at[j - 1], device)

    def lanes(value):
        partial = value[:, 0:128]
        for at in range(128, value.shape[1], 128):
            partial = partial + value[:, at:at + 128]
        return jnp.sum(partial, axis=0, keepdims=True)

    for step in range(PARTS + 0):
        if step < PARTS:
            for k in range(mine):
                s1(k, step)
        if step >= 0:
            for k in range(mine):
                s2(k, step - 0)
        if step == 1:
            select()
    for j in range(1, lines):
        gz_copy(j).wait_recv()
    for corner in range(PLANE):
        for k in range(mine):
            at = corner_band(k, corner)
            total = gz_ref[z, k, at]
            for j in range(1, lines):
                total = total + rz_ref[j - 1, k, at]
            tz_ref[corner, k] = total
    for j in range(1, PLANE):
        start(tz_copy(j))
    for j in range(1, PLANE):
        left_copy(j, q).start()
    for h in range(PARTS):
        for k in range(mine):
            s3(k, h)
    for j in range(1, PLANE):
        tz_copy(j).wait_recv()
    for k in range(mine):
        total = tz_ref[q, k]
        for j in range(1, PLANE):
            total = total + uz_ref[j - 1, k]
        own_ref[k, :, size - tail:size] = total.astype(BF16)

    p_ref[...] = jnp.zeros_like(p_ref)
    for k in range(mine):
        half = jnp.dot(own_ref[k], rsel_ref[k], preferred_element_type=F32).astype(BF16)
        for j in range(PLANE):
            hb_ref[j, k] = half[:, j * band:(j + 1) * band]
    for j in range(1, n_dp):
        half_copy(j, me).start()
    hall_ref[me] = hb_ref[q]
    for k in range(mine):
        value = own_ref[k].astype(F32)
        p_ref[mine + k:mine + k + 1, :] = lanes(value * value)
    for j in range(1, PLANE):
        left_copy(j, lax.rem(q + PLANE - j, PLANE)).wait_recv()
    for j in range(1, n_dp):
        half_copy(j, lax.rem(me + n_dp - j, n_dp)).wait_recv()
    for device in range(n_dp):
        line, corner = divmod(device, PLANE)
        for k in range(mine):
            a, b = (corner % 2, corner // 2) if k % 2 == 0 else (corner // 2, corner % 2)
            first = (a * 2 + b) * band + line * rows
            hfull_ref[k, first:first + rows, :] = hall_ref[device, k]
    for k in range(mine):
        square = jnp.zeros((1, 128), F32)
        for j in range(PLANE):
            value = jnp.dot(lband_ref[j, k], hfull_ref[k], preferred_element_type=F32)
            bo_ref[j, k] = value
            square = square + lanes(value * value)
        p_ref[k:k + 1, :] = square
    for j in range(1, n_dp):
        p_copy(j).start()
    for j in range(1, PLANE):
        both_copy(j, q).start()
    both_ref[core, q] = bo_ref[q]
    core_copy(0, core).start()
    total = p_ref[...]
    for j in range(1, n_dp):
        p_copy(j).wait_recv()
        total = total + pr_ref[j - 1]
    sum_ref[core] = total
    sum_mine, sum_theirs = sum_ref.at[core], sum_ref.at[other]
    remote(sum_mine, sum_mine, sum_send.at[0], sum_recv.at[0], core_mate).start()
    for j in range(1, PLANE):
        both_copy(j, lax.rem(q + PLANE - j, PLANE)).wait_recv()
        core_copy(j, core).start()
    for j in range(PLANE):
        core_copy(j, other).wait_recv()
    remote(sum_theirs, sum_theirs, sum_send.at[0], sum_recv.at[0], core_mate).wait_recv()

    factors = []
    for k in range(blocks):
        sums = jnp.sum(sum_ref[k // mine], axis=1, keepdims=True)
        at = k % mine
        factors.append(jnp.sqrt(sums[mine + at:mine + at + 1] / (sums[at:at + 1] + EPS)))
    for j in range(PLANE):
        part = slice(j * band, (j + 1) * band)
        grafted = [both_ref[k // mine, j, k % mine] * factors[k] for k in range(blocks)]
        moved = [(BETA * msel_ref[k, :, part] + grafted[k]).astype(BF16).astype(F32) for k in range(blocks)]
        for s in range(capacity):
            here = core * capacity + s
            value = BETA * mom_ref[here, :, part]
            update = jnp.zeros((rows, band), F32)
            for k in range(blocks):
                value = value + grafted[k] * hot(index[k], here)
                update = update + moved[k] * hot(target[k], here)
            mom_out[s, :, part] = value
            upd_out[s, :, part] = update.astype(BF16)
    for j in range(1, PLANE):
        left_copy(j, q).wait_send()
        both_copy(j, q).wait_send()
    for j in range(1, n_dp):
        half_copy(j, me).wait_send()
        p_copy(j).wait_send()
    for j in range(PLANE):
        core_copy(j, core).wait_send()
    remote(sum_mine, sum_mine, sum_send.at[0], sum_recv.at[0], core_mate).wait_send()
    for copy in sends:
        copy.wait_send()


def fused(n_dp, inputs_blk, grads_out, assign, param_owner, left_root, right_root, momentum):
    tokens, mine, size = inputs_blk.shape
    capacity = right_root.shape[0]
    blocks = assign.shape[0]
    rows = size // n_dp
    band, wing, lines = size // PLANE, size // 2, n_dp // PLANE
    slots = 2 * capacity
    vmem = pl.BlockSpec(memory_space=pltpu.VMEM)
    smem = pl.BlockSpec(memory_space=pltpu.SMEM)
    anyw = pl.BlockSpec(memory_space=pl.ANY)
    dma = pltpu.SemaphoreType.DMA
    flops = 2 * mine * tokens * size * size + 2 * blocks * size**3
    return pl.pallas_call(
        functools.partial(kernel, (n_dp, mine, blocks, capacity, size)),
        out_shape=(
            jax.ShapeDtypeStruct((capacity, rows, size), F32),
            jax.ShapeDtypeStruct((capacity, rows, size), BF16),
        ),
        in_specs=[vmem, vmem, smem, smem, anyw, anyw, anyw],
        out_specs=(vmem, vmem),
        scratch_shapes=[
            pltpu.VMEM((mine, tokens, wing), BF16),
            pltpu.VMEM((mine, tokens, size), BF16),
            pltpu.VMEM((mine, wing, size - size // 4), F32),
            pltpu.VMEM((mine, band, size), F32),
            pltpu.VMEM((mine, band, size), F32),
            pltpu.VMEM((mine, lines - 1, rows, size), F32),
            pltpu.VMEM((mine, rows, size), BF16),
            pltpu.VMEM((slots, size, size), BF16),
            pltpu.VMEM((slots, rows, size), BF16),
            pltpu.VMEM((slots, rows, size), F32),
            pltpu.VMEM((mine, size, size), BF16),
            pltpu.VMEM((PLANE, mine, rows, size), BF16),
            pltpu.VMEM((blocks, rows, size), F32),
            pltpu.VMEM((PLANE, mine, rows, band), BF16),
            pltpu.VMEM((n_dp, mine, rows, band), BF16),
            pltpu.VMEM((mine, size, band), BF16),
            pltpu.VMEM((PLANE, mine, rows, band), F32),
            pltpu.VMEM((2, PLANE, mine, rows, band), F32),
            pltpu.VMEM((8, 128), F32),
            pltpu.VMEM((n_dp - 1, 8, 128), F32),
            pltpu.VMEM((2, 8, 128), F32),
            dma((3,)), dma((3,)), dma((3,)),
            dma((mine,)), dma((mine,)),
            dma((mine, PARTS)), dma((mine, PARTS)),
            dma((mine, PARTS)), dma((mine, PARTS)),
            dma((mine, PARTS, lines - 1)), dma((mine, PARTS, lines - 1)),
            dma((PLANE - 1,)), dma((PLANE - 1,)),
            dma((n_dp - 1,)), dma((n_dp - 1,)),
            dma((PLANE - 1,)), dma((PLANE - 1,)),
            dma((PLANE,)), dma((PLANE,)),
            dma((n_dp - 1,)), dma((n_dp - 1,)),
            dma((1,)), dma((1,)),
            pltpu.VMEM((lines, mine, PLANE, rows, size // 4), F32),
            pltpu.VMEM((lines - 1, mine, PLANE, rows, size // 4), F32),
            pltpu.VMEM((PLANE, mine, rows, size // 4), F32),
            pltpu.VMEM((PLANE - 1, mine, rows, size // 4), F32),
            dma((lines - 1,)), dma((lines - 1,)),
            dma((PLANE - 1,)), dma((PLANE - 1,)),
        ],
        compiler_params=pltpu.CompilerParams(
            collective_id=0, has_side_effects=True, vmem_limit_bytes=40 * 1024 * 1024
        ),
        cost_estimate=pl.CostEstimate(flops=flops, bytes_accessed=4 * 1024 * 1024, transcendentals=0),
    )(
        inputs_blk.reshape(tokens, mine * size),
        grads_out.reshape(tokens, mine * size),
        assign, param_owner, left_root, right_root, momentum,
    )


def general(inputs_blk, grads_out, assign, param_owner, left_root, right_root, momentum):
    capacity = right_root.shape[0]
    blocks = assign.shape[0]
    my_index = lax.axis_index("mp")
    reduced = lax.psum_scatter(
        jnp.einsum("tkr,tkc->rkc", inputs_blk, grads_out, preferred_element_type=F32),
        "dp",
        scatter_dimension=0,
        tiled=True,
    )
    rounded = reduced.astype(BF16)
    gathered = lax.all_gather(rounded, "mp", axis=1, tiled=True)
    slot = slots_of(assign)
    slot_ids = lax.broadcasted_iota(jnp.int32, (capacity, blocks), 0)
    chooser = ((assign[None, :] == my_index) & (slot[None, :] == slot_ids)).astype(BF16)
    owned = jnp.einsum("ck,rkb->crb", chooser, gathered, preferred_element_type=F32).astype(BF16)
    half = jnp.einsum("crb,cbe->cre", owned, right_root, preferred_element_type=F32).astype(BF16)
    both = jnp.einsum(
        "cri,cie->cre",
        left_root,
        lax.all_gather(half, "dp", axis=1, tiled=True),
        preferred_element_type=F32,
    )
    grad_square = jnp.sum(jnp.square(owned.astype(F32)), axis=(1, 2))
    prec_square = jnp.sum(both * both, axis=(1, 2))
    grad_square, prec_square = lax.psum((grad_square, prec_square), "dp")
    factor = jnp.sqrt(grad_square / (prec_square + EPS))
    moved = BETA * momentum + both * factor[:, None, None]
    sending = moved.astype(BF16)
    pooled = lax.all_gather(sending, "mp", axis=0, tiled=True)
    place = slots_of(param_owner)
    source = assign * capacity + slot
    target_hot = ((param_owner[None, :] == my_index) & (place[None, :] == slot_ids)).astype(F32)
    pool_ids = lax.broadcasted_iota(jnp.int32, (blocks, pooled.shape[0]), 1)
    source_hot = (source[:, None] == pool_ids).astype(F32)
    mover = jnp.dot(target_hot, source_hot, preferred_element_type=F32).astype(BF16)
    update = jnp.einsum("qs,srb->qrb", mover, pooled, preferred_element_type=F32).astype(BF16)
    return (moved, update)


def solution(mesh):
    n_dp, n_mp = mesh.shape["dp"], mesh.shape["mp"]

    def on_device(inputs_blk, *rest):
        rows = inputs_blk.shape[2] // n_dp
        if n_mp == 2 and n_dp % PLANE == 0 and rows % 16 == 0 and inputs_blk.shape[1] == 2:
            return fused(n_dp, inputs_blk, *rest)
        return general(inputs_blk, *rest)

    placed = (
        P("dp", "mp", None),
        P("dp", "mp", None),
        P(),
        P(),
        P("mp", "dp", None),
        P("mp", None, None),
        P("mp", "dp", None),
    )
    return jax.shard_map(
        on_device,
        mesh=mesh,
        in_specs=placed,
        out_specs=(P("mp", "dp", None), P("mp", "dp", None)),
        check_vma=False,
    )
```
